256 devices in a mesh: row: 16 (over x, y), col: 16 (over z, core).
Axes of the slice: x: 4, y: 4, z: 8, core: 2. Of those that a mesh axis runs over, the one named last changes fastest.
Arguments:
- panel: float32 [131072, 256], P(('row', 'col')), may hold values from -1 to 1
- image_rest: float32 [131072, 256], P(('row', 'col')), may hold values from -300 to 300
- a_slab: float32 [131072, 2048], P('row', 'col'), may hold values from -288 to 288
Outputs:
- r_factor: float32 [256, 256], replicated
- slab_update: float32 [131072, 2048], P('row', 'col')
The draws below stay inside these ranges and needn't reach their ends.
All inputs are finite; a program needn't handle non-finite values.
Results may differ from the reference program's by a relative error of at most 0.000082.
Values sent between devices are 32-bit elements; how exact they have to be, the bound alone decides.
A program may use at most 128 MiB of HBM per device.

```python
import math
import jax
import jax.numpy as jnp
from jax import lax

PANEL = 256
SLAB = 2048
ORDER = 131072
ROWS_FLAT = 512
SLAB_DEV = 128
SLAB_ROWS = 8
N_COL = 16


def panel_values(key):
    keys = jax.random.split(key, 3)
    positions = jnp.arange(ORDER, dtype=jnp.float32)[:, None]
    ramp = 1.0 + 2.0 * positions / ORDER
    spread = jax.random.uniform(keys[0], (ORDER, 1), jnp.float32)
    row_scale = ramp * jnp.exp(spread * math.log(10.0)) / 10.0
    col_scale = jnp.exp(jax.random.uniform(keys[1], (1, PANEL), jnp.float32, math.log(0.3), math.log(3.0)))
    gauss = jnp.clip(jax.random.normal(keys[2], (ORDER, PANEL), jnp.float32), -6.0, 6.0)
    entries = gauss
    values = entries * row_scale * col_scale / math.sqrt(ORDER)
    return jnp.clip(values, -1.0, 1.0)


def draw_panel(key, part):
    values = panel_values(key)
    values = values.at[0, 0].set(1.0)
    values = values.at[ORDER - 1, PANEL - 1].set(-1.0)
    return values


def draw_image_rest(key, part):
    values = panel_values(key)
    key = jax.random.fold_in(key, 7)
    first, second, third = jax.random.split(key, 3)
    weights = jax.random.uniform(first, (1, PANEL), jnp.float32, 0.5, 1.5)
    signs = jnp.where(jax.random.bernoulli(second, 0.5, (1, PANEL)), 1.0, -1.0)
    noise = jax.random.normal(third, (ORDER, PANEL), jnp.float32)
    image_rest = 16.0 * math.sqrt(ORDER) * values * weights * signs + 8.0 * noise
    return jnp.clip(image_rest, -300.0, 300.0)


def shard_levels(stream_key, extent, shards, low, largest):
    gain, own = 1.0, jax.random.fold_in(stream_key, 6)
    for dim, blocks in shards:
        steps = jnp.exp(jax.random.uniform(jax.random.fold_in(own, dim), (blocks,), jnp.float32, low / len(shards), largest / len(shards)))
        gain = gain * jnp.repeat(steps, extent[dim] // blocks).reshape([-1 if axis == dim else 1 for axis in range(len(extent))])
    return gain


def centred(own_key, dims, scale, limit, pieces=(), kind=jnp.bfloat16):
    loudness = shard_levels(own_key, dims, pieces, -0.22, 0.18) if pieces else 1.0
    result = jax.random.normal(own_key, dims, jnp.float32) * scale * loudness
    return jnp.minimum(jnp.maximum(result, -limit), limit).astype(kind)


def setup_inputs(seed: int = 0) -> dict:
    streams_of = jax.random.split(jax.random.key(seed), 4)
    return {
        "panel": draw_panel(jax.random.fold_in(streams_of[3], 71), 0),
        "image_rest": draw_image_rest(jax.random.fold_in(streams_of[3], 71), 0),
        "a_slab": centred(streams_of[2], (ORDER, SLAB), 48.0, 288.0, ((0, 16), (1, 16)), jnp.float32),
    }


def slab_rows_of(matrix):
    position = jnp.arange(SLAB, dtype=jnp.int32)
    col_index = position // SLAB_DEV
    row_index = position % SLAB_DEV // SLAB_ROWS
    inner = position % SLAB_ROWS
    wanted = ((row_index * N_COL + col_index) * ROWS_FLAT + inner).astype(jnp.int32)
    return jnp.take(matrix, wanted, axis=0)

def reference(panel, image_rest, a_slab):
    highest = lax.Precision.HIGHEST
    gram_matrix = jnp.dot(panel.T.astype(jnp.float32), panel.astype(jnp.float32), precision=highest, preferred_element_type=jnp.float32)
    lower_factor = jnp.linalg.cholesky(gram_matrix)
    r_factor = lower_factor.T
    basis_rows = lax.linalg.triangular_solve(lower_factor, panel, left_side=False, lower=True, transpose_a=True)
    basis_slab = slab_rows_of(basis_rows)
    image_full = image_rest + 2.0 * jnp.dot(a_slab.astype(jnp.float32), basis_slab.astype(jnp.float32), precision=highest, preferred_element_type=jnp.float32)
    coupling = jnp.dot(basis_rows.T.astype(jnp.float32), image_full.astype(jnp.float32), precision=highest, preferred_element_type=jnp.float32)
    reduced = image_full - jnp.dot(basis_rows.astype(jnp.float32), coupling.astype(jnp.float32), precision=highest, preferred_element_type=jnp.float32)
    reduced_slab = slab_rows_of(reduced)
    slab_update = jnp.dot(basis_rows.astype(jnp.float32), reduced_slab.T.astype(jnp.float32), precision=highest, preferred_element_type=jnp.float32)
    slab_update = slab_update + jnp.dot(reduced.astype(jnp.float32), basis_slab.T.astype(jnp.float32), precision=highest, preferred_element_type=jnp.float32)
    return (r_factor, slab_update)
```

```python
import functools

import jax
import jax.numpy as jnp
from jax import lax
from jax.experimental import pallas as pl
from jax.experimental.pallas import tpu as pltpu
from jax.sharding import PartitionSpec as P

MESH = pl.DeviceIdType.MESH
HIGHEST = lax.Precision.HIGHEST
PIECE = 8


def dot(left, right, contract=((1,), (0,))):
    return lax.dot_general(
        left, right, (contract, ((), ())), precision=HIGHEST, preferred_element_type=jnp.float32
    )


def kernel(
    rows,
    chips,
    panel_hbm,
    rest_hbm,
    a_hbm,
    r_ref,
    out_hbm,
    a_buf,
    p_all,
    z_all,
    t_part,
    t_recv,
    rest,
    p_slab,
    z_slab,
    gram_src,
    gram_recv,
    gram_line,
    gram,
    coup_src,
    coup_recv,
    coup_line,
    coup,
    work,
    lower_inv,
    basis_slab_t,
    mix,
    staged,
    local_sem,
    a_local_sem,
    a_send_sem,
    a_recv_sem,
    plane_send_sem,
    plane_recv_sem,
    line_send_sem,
    line_recv_sem,
    ring_send_sem,
    ring_recv_sem,
    out_local_sem,
    out_send_sem,
    out_recv_sem,
):
    r = lax.axis_index("row")
    c = lax.axis_index("col")
    z = c // 2
    core = c % 2
    plane = 2 * rows
    q = core * rows + r
    half_ring = chips // 2
    half = p_all.shape[2]
    block = 2 * half
    width = p_all.shape[3]
    steps = chips - 1

    def chip(offset):
        return (z + offset + 2 * chips) % chips

    def at_plane(index):
        return (index % rows, 2 * z + index // rows)

    def at_chip(index):
        return (r, 2 * index + core)

    right, left = at_chip(chip(1)), at_chip(chip(-1))
    sibling = (r, 2 * z + (1 - core))

    panel_load = [
        pltpu.make_async_copy(
            panel_hbm.at[pl.ds(h * half, half)], p_all.at[z, h], local_sem.at[h]
        )
        for h in range(2)
    ]
    rest_load = [
        pltpu.make_async_copy(
            rest_hbm.at[pl.ds(h * half, half)], rest.at[h], local_sem.at[2 + h]
        )
        for h in range(2)
    ]

    def block_of(i):
        magnitude = half_ring - (i + 1) // 2
        sign = 1 - 2 * ((i + 1) % 2)
        return chip(jnp.where(i == 0, half_ring, magnitude * sign))

    def a_local(i):
        target = block_of(i)
        start = pl.multiple_of((2 * target + core) * block, block)
        return pltpu.make_async_copy(
            a_hbm.at[pl.ds(start, block)], a_buf.at[core, target], a_local_sem.at[i]
        )

    def a_remote(i):
        target = block_of(i)
        start = pl.multiple_of((2 * target + 1 - core) * block, block)
        return pltpu.make_async_remote_copy(
            src_ref=a_hbm.at[pl.ds(start, block)],
            dst_ref=a_buf.at[core, target],
            send_sem=a_send_sem.at[i],
            recv_sem=a_recv_sem.at[i],
            device_id=sibling,
            device_id_type=MESH,
        )

    for copy in panel_load + rest_load:
        copy.start()

    @pl.loop(0, chips)
    def _(i):
        a_local(i).start()

    barrier = pltpu.get_barrier_semaphore()

    @pl.loop(1, plane)
    def _(i):
        pl.semaphore_signal(
            barrier, inc=1, device_id=at_plane((q + i) % plane), device_id_type=MESH
        )

    @pl.loop(1, chips)
    def _(i):
        pl.semaphore_signal(barrier, inc=1, device_id=at_chip(chip(i)), device_id_type=MESH)

    pl.semaphore_wait(barrier, plane - 1 + chips - 1)

    def plane_copy(i, src, dst, slot):
        return pltpu.make_async_remote_copy(
            src_ref=src,
            dst_ref=dst,
            send_sem=plane_send_sem.at[slot],
            recv_sem=plane_recv_sem.at[slot],
            device_id=at_plane((q + i) % plane),
            device_id_type=MESH,
        )

    def plane_gather_start(src, dst, slot):
        @pl.loop(1, plane)
        def _(i):
            plane_copy(i, src, dst.at[q], slot).start()

    def plane_scatter_start(src, dst, slot):
        @pl.loop(1, plane)
        def _(i):
            plane_copy(i, src.at[(q + i) % plane], dst.at[q], slot).start()

    def plane_wait_recv(dst, slot):
        whole = dst.at[pl.ds(0, plane - 1)]
        pltpu.make_async_copy(whole, whole, plane_recv_sem.at[slot]).wait()

    def plane_wait_send(dst, slot):
        whole = dst.at[pl.ds(0, plane - 1)]
        pltpu.make_async_copy(whole, whole, plane_send_sem.at[slot]).wait()

    def line_start(buf, slot):
        @pl.loop(1, chips)
        def _(i):
            pltpu.make_async_remote_copy(
                src_ref=buf.at[z],
                dst_ref=buf.at[z],
                send_sem=line_send_sem.at[slot],
                recv_sem=line_recv_sem.at[slot],
                device_id=at_chip(chip(i)),
                device_id_type=MESH,
            ).start()

    def line_wait(buf, sem, slot):
        whole = buf.at[pl.ds(0, chips - 1)]
        pltpu.make_async_copy(whole, whole, sem.at[slot]).wait()

    def sum_first(ref, count):
        total = ref[0]
        for i in range(1, count):
            total = total + ref[i]
        return total

    def ring(kind, direction, n, src, dst):
        return pltpu.make_async_remote_copy(
            src_ref=src,
            dst_ref=dst,
            send_sem=ring_send_sem.at[kind, direction, n],
            recv_sem=ring_recv_sem.at[kind, direction, n],
            device_id=(right, left)[direction],
            device_id_type=MESH,
        )

    def gather_slot(direction, n, shift):
        away = n // 2 + shift
        h = (1 if n % 2 == 0 else 0) if direction == 0 else (0 if n % 2 == 0 else 1)
        return chip(-away if direction == 0 else away), h

    def gather_copy(buf, kind, direction, n):
        at, h = gather_slot(direction, n, 0)
        return ring(kind, direction, n, buf.at[at, h], buf.at[at, h])

    def gather_wait(buf, kind, direction, n):
        at, h = gather_slot(direction, n, 1)
        ring(kind, direction, n, buf.at[at, h], buf.at[at, h]).wait_recv()

    waited = set()

    def gather_need(buf, kind, direction, n):
        if (kind, direction, n) not in waited:
            waited.add((kind, direction, n))
            gather_wait(buf, kind, direction, n)

    def gather_send(buf, kind, n):
        if n >= steps:
            return
        for direction in range(2):
            if n >= 2:
                gather_need(buf, kind, direction, n - 2)
            gather_copy(buf, kind, direction, n).start()

    def sum_slot(direction, n):
        away = half_ring - (n + 1) // 2
        h = n % 2 if direction == 0 else 1 - n % 2
        return chip(away if direction == 0 else -away), h

    def sum_copy(direction, n):
        at, h = sum_slot(direction, n)
        return ring(1, direction, n, t_part.at[at, h], t_recv.at[direction, n])

    def sum_send(n):
        if n >= steps:
            return
        for direction in range(2):
            if n >= 2:
                sum_copy(direction, n - 2).wait_recv()
                at, h = sum_slot(direction, n)
                t_part[at, h] = t_part[at, h] + t_recv[direction, n - 2]
            sum_copy(direction, n).start()

    def panel_send(n):
        gather_send(p_all, 0, n)

    def image_send(n):
        gather_send(z_all, 2, n)

    for copy in panel_load:
        copy.wait()
    plane_gather_start(p_all.at[z, 0, pl.ds(0, PIECE)], p_slab, 0)

    @pl.loop(0, chips)
    def _(i):
        a_remote(i).start()

    panel_send(0)
    panel_send(1)
    p_slab[q] = p_all[z, 0, 0:PIECE]
    own = p_all[z].reshape(block, width)
    gram_src[...] = dot(own, own, ((0,), (0,))).reshape(gram_src.shape)
    plane_scatter_start(gram_src, gram_recv, 1)
    gram_recv[q] = gram_src[q]

    def partial_sums(i):
        target = block_of(i)
        a_local(i).wait()
        pltpu.make_async_remote_copy(
            src_ref=a_buf.at[1 - core, target],
            dst_ref=a_buf.at[1 - core, target],
            send_sem=a_send_sem.at[i],
            recv_sem=a_recv_sem.at[i],
            device_id=sibling,
            device_id_type=MESH,
        ).wait_recv()
        slab = p_slab[...].reshape(plane * PIECE, width)
        both = jnp.concatenate([a_buf[0, target], a_buf[1, target]], axis=1)
        t_part[target] = dot(both, slab).reshape(2, half, width)

    plane_wait_recv(p_slab, 0)
    partial_sums(0)
    sum_send(0)

    @pl.loop(1, 3)
    def _(i):
        partial_sums(i)

    sum_send(1)

    @pl.loop(3, chips)
    def _(i):
        partial_sums(i)

    plane_wait_recv(gram_recv, 1)
    gram_line[z] = sum_first(gram_recv, plane)
    line_start(gram_line, 0)
    panel_send(2)
    line_wait(gram_line, line_recv_sem, 0)
    gram[q] = sum_first(gram_line, chips)
    plane_gather_start(gram.at[q], gram, 2)

    nb = width // 2
    chunk = nb // 4

    def eliminate(first):
        size = nb - first
        lanes = lax.broadcasted_iota(jnp.int32, (1, nb), 1)
        sub = lax.broadcasted_iota(jnp.int32, (size, 1), 0) + first

        @pl.loop(first, first + chunk)
        def _(j):
            pivot_row = work[pl.ds(j, 1), :]
            pick = lanes == j
            pivot = jnp.sum(jnp.where(pick, pivot_row[:, :nb], 0.0), axis=1, keepdims=True)
            body = work[first:, :]
            column = jnp.sum(jnp.where(pick, body[:, :nb], 0.0), axis=1, keepdims=True)
            factor = jnp.where(sub > j, column / pivot, 0.0)
            work[first:, :] = body - factor * pivot_row

    def load_work(matrix):
        row_id = lax.broadcasted_iota(jnp.int32, (nb, nb), 0)
        col_id = lax.broadcasted_iota(jnp.int32, (nb, nb), 1)
        work[:, :nb] = matrix
        work[:, nb:] = jnp.where(row_id == col_id, 1.0, 0.0)

    def factors():
        row_id = lax.broadcasted_iota(jnp.int32, (nb, nb), 0)
        col_id = lax.broadcasted_iota(jnp.int32, (nb, nb), 1)
        upper = work[:, :nb]
        diagonal = jnp.sum(jnp.where(row_id == col_id, upper, 0.0), axis=1, keepdims=True)
        scale = 1.0 / jnp.sqrt(diagonal)
        return jnp.where(col_id >= row_id, upper * scale, 0.0), work[:, nb:] * scale

    sum_send(2)
    plane_wait_recv(gram, 2)
    gram_rows = gram_src.shape[1]
    whole_gram = gram[...].reshape(plane * gram_rows, width)
    load_work(whole_gram[:nb, :nb])
    eliminate(0)
    sum_send(3)
    eliminate(chunk)
    panel_send(3)
    eliminate(2 * chunk)
    sum_send(4)
    eliminate(3 * chunk)
    upper_a, inverse_a = factors()
    r_ref[:nb, :nb] = upper_a
    lower_inv[:nb, :nb] = inverse_a
    whole_gram = gram[...].reshape(plane * gram_rows, width)
    cross = dot(inverse_a, whole_gram[:nb, nb:])
    r_ref[:nb, nb:] = cross
    r_ref[nb:, :nb] = jnp.zeros((nb, nb), jnp.float32)
    lower_inv[:nb, nb:] = jnp.zeros((nb, nb), jnp.float32)
    load_work(whole_gram[nb:, nb:] - dot(cross, cross, ((0,), (0,))))
    sum_send(5)
    eliminate(0)
    panel_send(4)
    eliminate(chunk)
    sum_send(6)
    eliminate(2 * chunk)
    panel_send(5)
    eliminate(3 * chunk)
    upper_b, inverse_b = factors()
    r_ref[nb:, nb:] = upper_b
    lower_inv[nb:, nb:] = inverse_b
    lower_inv[nb:, :nb] = -dot(inverse_b, dot(r_ref[:nb, nb:], lower_inv[:nb, :nb], ((0,), (0,))))

    inverse = lower_inv[...]
    basis_slab_t[...] = dot(
        inverse, p_slab[...].reshape(plane * PIECE, width), ((1,), (1,))
    )
    own_basis = dot(p_all[z].reshape(block, width), inverse, ((1,), (1,)))

    for copy in rest_load:
        copy.wait()
    for direction in range(2):
        for n in (steps - 2, steps - 1):
            sum_copy(direction, n).wait_recv()
    for h in range(2):
        first = t_recv[0, steps - 2 if h == 1 else steps - 1]
        second = t_recv[1, steps - 2 if h == 0 else steps - 1]
        total = t_part[z, h] + first + second
        z_all[z, h] = rest[h] + 2.0 * dot(total, inverse, ((1,), (1,)))
    image_send(0)
    image_send(1)
    plane_gather_start(z_all.at[z, 0, pl.ds(0, PIECE)], z_slab, 3)
    z_slab[q] = z_all[z, 0, 0:PIECE]
    coup_src[...] = dot(
        own_basis, z_all[z].reshape(block, width), ((0,), (0,))
    ).reshape(coup_src.shape)
    plane_scatter_start(coup_src, coup_recv, 4)
    coup_recv[q] = coup_src[q]
    panel_send(6)
    plane_wait_recv(coup_recv, 4)
    coup_line[z] = sum_first(coup_recv, plane)
    line_start(coup_line, 1)
    image_send(2)
    line_wait(coup_line, line_recv_sem, 1)
    coup[q] = sum_first(coup_line, chips)
    plane_gather_start(coup.at[q], coup, 5)
    image_send(3)
    plane_wait_recv(z_slab, 3)
    plane_wait_recv(coup, 5)
    coupling = coup[...].reshape(width, width)
    slab_t = basis_slab_t[...]
    inner = jnp.transpose(z_slab[...].reshape(plane * PIECE, width))
    inner = inner - dot(coupling, slab_t) - dot(coupling, slab_t, ((0,), (0,)))
    mix[...] = dot(lower_inv[...], inner, ((0,), (0,)))

    columns = plane * PIECE // 2

    def out_copies(slot, at, h):
        start = pl.multiple_of((2 * at + core) * block + h * half, half)
        local = pltpu.make_async_copy(
            staged.at[slot, core], out_hbm.at[pl.ds(start, half)], out_local_sem.at[slot]
        )
        remote = pltpu.make_async_remote_copy(
            src_ref=staged.at[slot, 1 - core],
            dst_ref=out_hbm.at[pl.ds(start, half)],
            send_sem=out_send_sem.at[slot],
            recv_sem=out_recv_sem.at[slot],
            device_id=sibling,
            device_id_type=MESH,
        )
        return local, remote

    done = []

    def update(at, h):
        slot = len(done)
        value = dot(p_all[at, h], mix[...]) + dot(z_all[at, h], basis_slab_t[...])
        staged[slot, 0] = value[:, :columns]
        staged[slot, 1] = value[:, columns:]
        local, remote = out_copies(slot, at, h)
        local.start()
        remote.start()
        done.append((at, h))

    update(z, 0)
    update(z, 1)
    sent = 4
    for n in range(steps):
        if sent < steps:
            image_send(sent)
            sent += 1
        for direction in range(2):
            gather_need(z_all, 2, direction, n)
            gather_need(p_all, 0, direction, n)
            update(*gather_slot(direction, n, 1))

    for slot, (at, h) in enumerate(done):
        local, remote = out_copies(slot, at, h)
        local.wait()
        remote.wait_send()
        other = pl.multiple_of((2 * at + 1 - core) * block + h * half, half)
        pltpu.make_async_remote_copy(
            src_ref=staged.at[slot, core],
            dst_ref=out_hbm.at[pl.ds(other, half)],
            send_sem=out_send_sem.at[slot],
            recv_sem=out_recv_sem.at[slot],
            device_id=sibling,
            device_id_type=MESH,
        ).wait_recv()

    for direction in range(2):
        for n in range(steps):
            gather_copy(p_all, 0, direction, n).wait_send()
            sum_copy(direction, n).wait_send()
            gather_copy(z_all, 2, direction, n).wait_send()

    @pl.loop(0, chips)
    def _(i):
        a_remote(i).wait_send()

    plane_wait_send(p_slab, 0)
    plane_wait_send(gram_recv, 1)
    plane_wait_send(gram, 2)
    plane_wait_send(z_slab, 3)
    plane_wait_send(coup_recv, 4)
    plane_wait_send(coup, 5)
    line_wait(gram_line, line_send_sem, 0)
    line_wait(coup_line, line_send_sem, 1)


def per_device(panel, image_rest, a_slab):
    f32 = jnp.float32
    rows = lax.axis_size("row")
    chips = lax.axis_size("col") // 2
    block, width = panel.shape
    columns = a_slab.shape[1]
    half = block // 2
    plane = 2 * rows
    gram_rows = width // plane
    slab = plane * PIECE
    steps = chips - 1
    dma = pltpu.SemaphoreType.DMA
    hbm = pl.BlockSpec(memory_space=pltpu.HBM)
    vmem = pl.BlockSpec(memory_space=pltpu.VMEM)
    reduction = [
        pltpu.VMEM((plane, gram_rows, width), f32),
        pltpu.VMEM((plane, gram_rows, width), f32),
        pltpu.VMEM((chips, gram_rows, width), f32),
        pltpu.VMEM((plane, gram_rows, width), f32),
    ]
    return pl.pallas_call(
        functools.partial(kernel, rows, chips),
        out_shape=(
            jax.ShapeDtypeStruct((width, width), f32),
            jax.ShapeDtypeStruct(a_slab.shape, f32),
        ),
        in_specs=[hbm, hbm, hbm],
        out_specs=(vmem, hbm),
        scratch_shapes=[
            pltpu.VMEM((2, chips, block, columns), f32),
            pltpu.VMEM((chips, 2, half, width), f32),
            pltpu.VMEM((chips, 2, half, width), f32),
            pltpu.VMEM((chips, 2, half, width), f32),
            pltpu.VMEM((2, steps, half, width), f32),
            pltpu.VMEM((2, half, width), f32),
            pltpu.VMEM((plane, PIECE, width), f32),
            pltpu.VMEM((plane, PIECE, width), f32),
            *reduction,
            *reduction,
            pltpu.VMEM((width // 2, width), f32),
            pltpu.VMEM((width, width), f32),
            pltpu.VMEM((width, slab), f32),
            pltpu.VMEM((width, slab), f32),
            pltpu.VMEM((2 * chips, 2, half, columns), f32),
            dma((4,)),
            dma((chips,)),
            dma((chips,)),
            dma((chips,)),
            dma((6,)),
            dma((6,)),
            dma((2,)),
            dma((2,)),
            dma((3, 2, steps)),
            dma((3, 2, steps)),
            dma((2 * chips,)),
            dma((2 * chips,)),
            dma((2 * chips,)),
        ],
        compiler_params=pltpu.CompilerParams(
            collective_id=0, has_side_effects=True, vmem_limit_bytes=56 * 1024 * 1024
        ),
    )(panel, image_rest, a_slab)


def solution(mesh):
    placed = (P(("row", "col"), None), P(("row", "col"), None), P("row", "col"))
    return jax.shard_map(
        per_device, mesh=mesh, in_specs=placed, out_specs=(P(), P("row", "col")), check_vma=False
    )
```

```python
import functools

import jax
import jax.numpy as jnp
from jax import lax
from jax.experimental import pallas as pl
from jax.experimental.pallas import tpu as pltpu
from jax.sharding import PartitionSpec as P

MESH = pl.DeviceIdType.MESH
HIGHEST = lax.Precision.HIGHEST
PIECE = 8


def dot(left, right, contract=((1,), (0,))):
    return lax.dot_general(
        left, right, (contract, ((), ())), precision=HIGHEST, preferred_element_type=jnp.float32
    )


def kernel(
    rows,
    chips,
    panel_hbm,
    rest_hbm,
    a_hbm,
    r_ref,
    out_ref,
    a_buf,
    p_all,
    z_all,
    t_part,
    t_recv,
    rest,
    p_slab,
    z_slab,
    p_side,
    z_side,
    gram_src,
    gram_recv,
    gram_line,
    gram,
    coup_src,
    coup_recv,
    coup_line,
    coup,
    work,
    lower_inv,
    basis_slab_t,
    mix,
    staged,
    passed,
    local_sem,
    a_local_sem,
    a_send_sem,
    a_recv_sem,
    plane_send_sem,
    plane_recv_sem,
    line_send_sem,
    line_recv_sem,
    ring_send_sem,
    ring_recv_sem,
    side_send_sem,
    side_recv_sem,
    out_send_sem,
    out_recv_sem,
    pass_send_sem,
    pass_recv_sem,
):
    r = lax.axis_index("row")
    c = lax.axis_index("col")
    z = c // 2
    core = c % 2
    plane = 2 * rows
    q = core * rows + r
    half_ring = chips // 2
    half = p_all.shape[2]
    block = 2 * half
    width = p_all.shape[3]
    steps = chips - 1

    def chip(offset):
        return (z + offset + 2 * chips) % chips

    def at_plane(index):
        return (index % rows, 2 * z + index // rows)

    def at_chip(index):
        return (r, 2 * index + core)

    right, left = at_chip(chip(1)), at_chip(chip(-1))
    sibling = (r, 2 * z + (1 - core))

    panel_load = [
        pltpu.make_async_copy(
            panel_hbm.at[pl.ds(h * half, half)], p_all.at[z, h], local_sem.at[h]
        )
        for h in range(2)
    ]
    rest_load = [
        pltpu.make_async_copy(
            rest_hbm.at[pl.ds(h * half, half)], rest.at[h], local_sem.at[2 + h]
        )
        for h in range(2)
    ]

    def block_of(i):
        magnitude = half_ring - (i + 1) // 2
        sign = 1 - 2 * ((i + 1) % 2)
        return chip(jnp.where(i == 0, half_ring, magnitude * sign))

    def a_local(i):
        target = block_of(i)
        start = pl.multiple_of((2 * target + core) * block, block)
        return pltpu.make_async_copy(
            a_hbm.at[pl.ds(start, block)], a_buf.at[core, target], a_local_sem.at[i]
        )

    def a_remote(i):
        target = block_of(i)
        start = pl.multiple_of((2 * target + 1 - core) * block, block)
        return pltpu.make_async_remote_copy(
            src_ref=a_hbm.at[pl.ds(start, block)],
            dst_ref=a_buf.at[core, target],
            send_sem=a_send_sem.at[i],
            recv_sem=a_recv_sem.at[i],
            device_id=sibling,
            device_id_type=MESH,
        )

    for copy in panel_load + rest_load:
        copy.start()

    @pl.loop(0, chips)
    def _(i):
        a_local(i).start()

    barrier = pltpu.get_barrier_semaphore()

    @pl.loop(1, plane)
    def _(i):
        pl.semaphore_signal(
            barrier, inc=1, device_id=at_plane((q + i) % plane), device_id_type=MESH
        )

    @pl.loop(1, chips)
    def _(i):
        pl.semaphore_signal(barrier, inc=1, device_id=at_chip(chip(i)), device_id_type=MESH)

    for copy in panel_load:
        copy.wait()
    pl.semaphore_wait(barrier, plane - 1 + chips - 1)

    def plane_copy(i, src, dst, slot):
        return pltpu.make_async_remote_copy(
            src_ref=src,
            dst_ref=dst,
            send_sem=plane_send_sem.at[slot],
            recv_sem=plane_recv_sem.at[slot],
            device_id=at_plane((q + i) % plane),
            device_id_type=MESH,
        )

    def side_copy(kind, direction, src, dst):
        return pltpu.make_async_remote_copy(
            src_ref=src,
            dst_ref=dst.at[q, 1 - direction],
            send_sem=side_send_sem.at[kind, direction],
            recv_sem=side_recv_sem.at[kind, direction],
            device_id=(right, left)[direction],
            device_id_type=MESH,
        )

    def plane_gather_start(src, dst, slot):
        @pl.loop(1, plane)
        def _(i):
            plane_copy(i, src, dst.at[q], slot).start()

    def plane_scatter_start(src, dst, slot):
        @pl.loop(1, plane)
        def _(i):
            plane_copy(i, src.at[(q + i) % plane], dst.at[q], slot).start()

    def plane_wait_recv(dst, slot):
        whole = dst.at[pl.ds(0, plane - 1)]
        pltpu.make_async_copy(whole, whole, plane_recv_sem.at[slot]).wait()

    def plane_wait_send(dst, slot):
        whole = dst.at[pl.ds(0, plane - 1)]
        pltpu.make_async_copy(whole, whole, plane_send_sem.at[slot]).wait()

    def line_start(buf, slot):
        @pl.loop(1, chips)
        def _(i):
            pltpu.make_async_remote_copy(
                src_ref=buf.at[z],
                dst_ref=buf.at[z],
                send_sem=line_send_sem.at[slot],
                recv_sem=line_recv_sem.at[slot],
                device_id=at_chip(chip(i)),
                device_id_type=MESH,
            ).start()

    def line_wait(buf, sem, slot):
        whole = buf.at[pl.ds(0, chips - 1)]
        pltpu.make_async_copy(whole, whole, sem.at[slot]).wait()

    def sum_first(ref, count):
        total = ref[0]
        for i in range(1, count):
            total = total + ref[i]
        return total

    def ring(kind, direction, n, src, dst):
        return pltpu.make_async_remote_copy(
            src_ref=src,
            dst_ref=dst,
            send_sem=ring_send_sem.at[kind, direction, n],
            recv_sem=ring_recv_sem.at[kind, direction, n],
            device_id=(right, left)[direction],
            device_id_type=MESH,
        )

    def gather_slot(direction, n, shift):
        away = n // 2 + shift
        h = (1 if n % 2 == 0 else 0) if direction == 0 else (0 if n % 2 == 0 else 1)
        return chip(-away if direction == 0 else away), h

    def gather_copy(buf, kind, direction, n):
        at, h = gather_slot(direction, n, 0)
        return ring(kind, direction, n, buf.at[at, h], buf.at[at, h])

    def gather_wait(buf, kind, direction, n):
        at, h = gather_slot(direction, n, 1)
        ring(kind, direction, n, buf.at[at, h], buf.at[at, h]).wait_recv()

    waited = set()

    def gather_need(buf, kind, direction, n):
        if n >= 0 and (kind, direction, n) not in waited:
            waited.add((kind, direction, n))
            gather_wait(buf, kind, direction, n)

    def gather_send(buf, kind, n):
        if n >= steps - 2:
            return
        for direction in range(2):
            if n >= 2:
                gather_need(buf, kind, direction, n - 2)
            gather_copy(buf, kind, direction, n).start()

    def sum_slot(direction, n):
        away = half_ring - (n + 1) // 2
        h = n % 2 if direction == 0 else 1 - n % 2
        return chip(away if direction == 0 else -away), h

    def sum_copy(direction, n):
        at, h = sum_slot(direction, n)
        return ring(1, direction, n, t_part.at[at, h], t_recv.at[direction, n])

    def sum_send(n):
        if n >= steps:
            return
        for direction in range(2):
            if n >= 2:
                sum_copy(direction, n - 2).wait_recv()
                at, h = sum_slot(direction, n)
                t_part[at, h] = t_part[at, h] + t_recv[direction, n - 2]
            sum_copy(direction, n).start()

    def panel_send(n):
        gather_send(p_all, 0, n)

    def image_send(n):
        gather_send(z_all, 2, n)

    for direction in range(2):
        side_copy(0, direction, p_all.at[z, 0, pl.ds(0, PIECE)], p_side).start()
    panel_send(0)
    plane_gather_start(p_all.at[z, 0, pl.ds(0, PIECE)], p_slab, 0)

    @pl.loop(0, chips)
    def _(i):
        a_remote(i).start()

    panel_send(1)
    p_slab[q] = p_all[z, 0, 0:PIECE]
    own = p_all[z].reshape(block, width)
    gram_src[...] = dot(own, own, ((0,), (0,))).reshape(gram_src.shape)
    plane_scatter_start(gram_src, gram_recv, 1)
    gram_recv[q] = gram_src[q]

    def partial_sums(i):
        target = block_of(i)
        a_local(i).wait()
        pltpu.make_async_remote_copy(
            src_ref=a_buf.at[1 - core, target],
            dst_ref=a_buf.at[1 - core, target],
            send_sem=a_send_sem.at[i],
            recv_sem=a_recv_sem.at[i],
            device_id=sibling,
            device_id_type=MESH,
        ).wait_recv()
        slab = p_slab[...].reshape(plane * PIECE, width)
        both = jnp.concatenate([a_buf[0, target], a_buf[1, target]], axis=1)
        t_part[target] = dot(both, slab).reshape(2, half, width)

    plane_wait_recv(p_slab, 0)
    partial_sums(0)
    sum_send(0)

    @pl.loop(1, 3)
    def _(i):
        partial_sums(i)

    sum_send(1)

    @pl.loop(3, chips)
    def _(i):
        partial_sums(i)

    plane_wait_recv(gram_recv, 1)
    gram_line[z] = sum_first(gram_recv, plane)
    line_start(gram_line, 0)
    panel_send(2)
    line_wait(gram_line, line_recv_sem, 0)
    gram[q] = sum_first(gram_line, chips)
    plane_gather_start(gram.at[q], gram, 2)

    nb = width // 2
    chunk = nb // 4

    def eliminate(first):
        size = nb - first
        lanes = lax.broadcasted_iota(jnp.int32, (1, nb), 1)
        sub = lax.broadcasted_iota(jnp.int32, (size, 1), 0) + first

        @pl.loop(first, first + chunk)
        def _(j):
            pivot_row = work[pl.ds(j, 1), :]
            pick = lanes == j
            pivot = jnp.sum(jnp.where(pick, pivot_row[:, :nb], 0.0), axis=1, keepdims=True)
            body = work[first:, :]
            column = jnp.sum(jnp.where(pick, body[:, :nb], 0.0), axis=1, keepdims=True)
            factor = jnp.where(sub > j, column / pivot, 0.0)
            work[first:, :] = body - factor * pivot_row

    def load_work(matrix):
        row_id = lax.broadcasted_iota(jnp.int32, (nb, nb), 0)
        col_id = lax.broadcasted_iota(jnp.int32, (nb, nb), 1)
        work[:, :nb] = matrix
        work[:, nb:] = jnp.where(row_id == col_id, 1.0, 0.0)

    def factors():
        row_id = lax.broadcasted_iota(jnp.int32, (nb, nb), 0)
        col_id = lax.broadcasted_iota(jnp.int32, (nb, nb), 1)
        upper = work[:, :nb]
        diagonal = jnp.sum(jnp.where(row_id == col_id, upper, 0.0), axis=1, keepdims=True)
        scale = 1.0 / jnp.sqrt(diagonal)
        return jnp.where(col_id >= row_id, upper * scale, 0.0), work[:, nb:] * scale

    for direction in range(2):
        side_copy(0, direction, p_all.at[z, 0, pl.ds(0, PIECE)], p_side).wait_recv()
    plane_gather_start(p_side.at[q], p_side, 6)
    plane_wait_recv(gram, 2)
    gram_rows = gram_src.shape[1]
    whole_gram = gram[...].reshape(plane * gram_rows, width)
    load_work(whole_gram[:nb, :nb])
    eliminate(0)
    sum_send(2)
    panel_send(3)
    eliminate(chunk)
    eliminate(2 * chunk)
    sum_send(3)
    eliminate(3 * chunk)
    upper_a, inverse_a = factors()
    r_ref[:nb, :nb] = upper_a
    lower_inv[:nb, :nb] = inverse_a
    whole_gram = gram[...].reshape(plane * gram_rows, width)
    cross = dot(inverse_a, whole_gram[:nb, nb:])
    r_ref[:nb, nb:] = cross
    r_ref[nb:, :nb] = jnp.zeros((nb, nb), jnp.float32)
    lower_inv[:nb, nb:] = jnp.zeros((nb, nb), jnp.float32)
    load_work(whole_gram[nb:, nb:] - dot(cross, cross, ((0,), (0,))))
    sum_send(4)
    eliminate(0)
    eliminate(chunk)
    sum_send(5)
    eliminate(2 * chunk)
    eliminate(3 * chunk)
    upper_b, inverse_b = factors()
    r_ref[nb:, nb:] = upper_b
    lower_inv[nb:, nb:] = inverse_b
    lower_inv[nb:, :nb] = -dot(inverse_b, dot(r_ref[:nb, nb:], lower_inv[:nb, :nb], ((0,), (0,))))
    sum_send(6)
    panel_send(4)

    slab = plane * PIECE
    inverse = lower_inv[...]
    plane_wait_recv(p_side, 6)

    def columns_of(i):
        return slice(i * slab, (i + 1) * slab)

    def three(own_rows, side):
        return (
            own_rows[...].reshape(slab, width),
            side[:, 0].reshape(slab, width),
            side[:, 1].reshape(slab, width),
        )

    for i, slab_rows in enumerate(three(p_slab, p_side)):
        basis_slab_t[:, columns_of(i)] = dot(inverse, slab_rows, ((1,), (1,)))
    own_basis = dot(p_all[z].reshape(block, width), inverse, ((1,), (1,)))

    for copy in rest_load:
        copy.wait()
    for direction in range(2):
        for n in (steps - 2, steps - 1):
            sum_copy(direction, n).wait_recv()
    for h in range(2):
        first = t_recv[0, steps - 2 if h == 1 else steps - 1]
        second = t_recv[1, steps - 2 if h == 0 else steps - 1]
        total = t_part[z, h] + first + second
        z_all[z, h] = rest[h] + 2.0 * dot(total, inverse, ((1,), (1,)))
    for direction in range(2):
        side_copy(1, direction, z_all.at[z, 0, pl.ds(0, PIECE)], z_side).start()
    image_send(0)
    image_send(1)
    coup_src[...] = dot(
        own_basis, z_all[z].reshape(block, width), ((0,), (0,))
    ).reshape(coup_src.shape)
    plane_scatter_start(coup_src, coup_recv, 4)
    coup_recv[q] = coup_src[q]
    plane_gather_start(z_all.at[z, 0, pl.ds(0, PIECE)], z_slab, 3)
    z_slab[q] = z_all[z, 0, 0:PIECE]
    plane_wait_recv(coup_recv, 4)
    coup_line[z] = sum_first(coup_recv, plane)
    line_start(coup_line, 1)
    for direction in range(2):
        side_copy(1, direction, z_all.at[z, 0, pl.ds(0, PIECE)], z_side).wait_recv()
    plane_gather_start(z_side.at[q], z_side, 7)
    image_send(2)
    line_wait(coup_line, line_recv_sem, 1)
    coup[q] = sum_first(coup_line, chips)
    plane_gather_start(coup.at[q], coup, 5)
    plane_wait_recv(z_slab, 3)
    plane_wait_recv(z_side, 7)
    plane_wait_recv(coup, 5)
    image_send(3)
    coupling = coup[...].reshape(width, width)
    for i, slab_rows in enumerate(three(z_slab, z_side)):
        slab_t = basis_slab_t[:, columns_of(i)]
        inner = jnp.transpose(slab_rows)
        inner = inner - dot(coupling, slab_t) - dot(coupling, slab_t, ((0,), (0,)))
        mix[:, columns_of(i)] = dot(lower_inv[...], inner, ((0,), (0,)))

    columns = slab // 2

    def first_row(at, core_of_rows, h):
        return pl.multiple_of((2 * at + core_of_rows) * block + h * half, half)

    def update_block(at, h, i):
        value = dot(p_all[at, h], mix[:, columns_of(i)])
        value = value + dot(z_all[at, h], basis_slab_t[:, columns_of(i)])
        return value[:, :columns], value[:, columns:]

    def swap_copy(slot, start):
        return pltpu.make_async_remote_copy(
            src_ref=staged.at[slot],
            dst_ref=out_ref.at[pl.ds(start, half)],
            send_sem=out_send_sem.at[slot],
            recv_sem=out_recv_sem.at[slot],
            device_id=sibling,
            device_id_type=MESH,
        )

    done = []

    def update(at, h):
        slot = len(done)
        low, high = update_block(at, h, 0)
        staged[slot] = jnp.where(core == 0, high, low)
        start = first_row(at, core, h)
        swap_copy(slot, start).start()
        out_ref[pl.ds(start, half), :] = jnp.where(core == 0, low, high)
        done.append((at, h))

    def pass_copy(direction, n, source, target, at, h):
        return pltpu.make_async_remote_copy(
            src_ref=passed.at[direction, n, target],
            dst_ref=out_ref.at[pl.ds(first_row(at, source, h), half)],
            send_sem=pass_send_sem.at[direction, n, target],
            recv_sem=pass_recv_sem.at[direction, n, source],
            device_id=(r, 2 * chip(1 if direction == 0 else -1) + target),
            device_id_type=MESH,
        )

    def pass_send(n):
        for direction in range(2):
            last = steps - 2 + n
            gather_need(z_all, 2, direction, last - 2)
            gather_need(p_all, 0, direction, last - 2)
            at, h = gather_slot(direction, last, 0)
            low, high = update_block(at, h, 1 + direction)
            passed[direction, n, 0] = low
            passed[direction, n, 1] = high
            for target in range(2):
                pass_copy(direction, n, core, target, at, h).start()

    def update_received(n):
        for direction in range(2):
            gather_need(z_all, 2, direction, n)
            gather_need(p_all, 0, direction, n)
            update(*gather_slot(direction, n, 1))

    image_send(4)
    update(z, 0)
    update(z, 1)
    for n in range(steps - 4):
        update_received(n)
    pass_send(0)
    pass_send(1)
    for n in range(max(steps - 4, 0), steps - 2):
        update_received(n)

    for slot, (at, h) in enumerate(done):
        swap_copy(slot, first_row(at, core, h)).wait_send()
        swap_copy(slot, first_row(at, 1 - core, h)).wait_recv()
    for n in range(2):
        for direction in range(2):
            last = steps - 2 + n
            for index in range(2):
                at, h = gather_slot(direction, last, 0)
                pass_copy(direction, n, core, index, at, h).wait_send()
                at, h = gather_slot(direction, last, 1)
                pass_copy(direction, n, index, index, at, h).wait_recv()

    for direction in range(2):
        for n in range(steps):
            sum_copy(direction, n).wait_send()
        for n in range(steps - 2):
            gather_copy(p_all, 0, direction, n).wait_send()
            gather_copy(z_all, 2, direction, n).wait_send()
        side_copy(0, direction, p_all.at[z, 0, pl.ds(0, PIECE)], p_side).wait_send()
        side_copy(1, direction, z_all.at[z, 0, pl.ds(0, PIECE)], z_side).wait_send()

    @pl.loop(0, chips)
    def _(i):
        a_remote(i).wait_send()

    plane_wait_send(p_slab, 0)
    plane_wait_send(gram_recv, 1)
    plane_wait_send(gram, 2)
    plane_wait_send(z_slab, 3)
    plane_wait_send(coup_recv, 4)
    plane_wait_send(coup, 5)
    plane_wait_send(p_side, 6)
    plane_wait_send(z_side, 7)
    line_wait(gram_line, line_send_sem, 0)
    line_wait(coup_line, line_send_sem, 1)


def per_device(panel, image_rest, a_slab):
    f32 = jnp.float32
    rows = lax.axis_size("row")
    chips = lax.axis_size("col") // 2
    block, width = panel.shape
    columns = a_slab.shape[1]
    half = block // 2
    plane = 2 * rows
    gram_rows = width // plane
    slab = plane * PIECE
    steps = chips - 1
    dma = pltpu.SemaphoreType.DMA
    hbm = pl.BlockSpec(memory_space=pltpu.HBM)
    vmem = pl.BlockSpec(memory_space=pltpu.VMEM)
    reduction = [
        pltpu.VMEM((plane, gram_rows, width), f32),
        pltpu.VMEM((plane, gram_rows, width), f32),
        pltpu.VMEM((chips, gram_rows, width), f32),
        pltpu.VMEM((plane, gram_rows, width), f32),
    ]
    return pl.pallas_call(
        functools.partial(kernel, rows, chips),
        out_shape=(
            pltpu.VMEM((width, width), f32),
            pltpu.VMEM(a_slab.shape, f32),
        ),
        in_specs=[hbm, hbm, hbm],
        out_specs=(vmem, vmem),
        scratch_shapes=[
            pltpu.VMEM((2, chips, block, columns), f32),
            pltpu.VMEM((chips, 2, half, width), f32),
            pltpu.VMEM((chips, 2, half, width), f32),
            pltpu.VMEM((chips, 2, half, width), f32),
            pltpu.VMEM((2, steps, half, width), f32),
            pltpu.VMEM((2, half, width), f32),
            pltpu.VMEM((plane, PIECE, width), f32),
            pltpu.VMEM((plane, PIECE, width), f32),
            pltpu.VMEM((plane, 2, PIECE, width), f32),
            pltpu.VMEM((plane, 2, PIECE, width), f32),
            *reduction,
            *reduction,
            pltpu.VMEM((width // 2, width), f32),
            pltpu.VMEM((width, width), f32),
            pltpu.VMEM((width, 3 * slab), f32),
            pltpu.VMEM((width, 3 * slab), f32),
            pltpu.VMEM((2 * chips - 4, half, columns), f32),
            pltpu.VMEM((2, 2, 2, half, columns), f32),
            dma((4,)),
            dma((chips,)),
            dma((chips,)),
            dma((chips,)),
            dma((8,)),
            dma((8,)),
            dma((2,)),
            dma((2,)),
            dma((3, 2, steps)),
            dma((3, 2, steps)),
            dma((2, 2)),
            dma((2, 2)),
            dma((2 * chips - 4,)),
            dma((2 * chips - 4,)),
            dma((2, 2, 2)),
            dma((2, 2, 2)),
        ],
        compiler_params=pltpu.CompilerParams(
            collective_id=0, has_side_effects=True, vmem_limit_bytes=56 * 1024 * 1024
        ),
    )(panel, image_rest, a_slab)


def solution(mesh):
    placed = (P(("row", "col"), None), P(("row", "col"), None), P("row", "col"))
    return jax.shard_map(
        per_device, mesh=mesh, in_specs=placed, out_specs=(P(), P("row", "col")), check_vma=False
    )
```

```python
import functools

import jax
import jax.numpy as jnp
from jax import lax
from jax.experimental import pallas as pl
from jax.experimental.pallas import tpu as pltpu
from jax.sharding import PartitionSpec as P

MESH = pl.DeviceIdType.MESH
HIGHEST = lax.Precision.HIGHEST
PIECE = 8


def dot(left, right, contract=((1,), (0,))):
    return lax.dot_general(
        left, right, (contract, ((), ())), precision=HIGHEST, preferred_element_type=jnp.float32
    )


def kernel(
    rows,
    chips,
    panel_hbm,
    rest_hbm,
    a_hbm,
    r_ref,
    out_ref,
    a_buf,
    p_all,
    z_all,
    t_part,
    t_recv,
    rest,
    p_slab,
    z_slab,
    p_side,
    z_side,
    gram_src,
    gram_recv,
    gram_line,
    gram,
    coup_src,
    coup_recv,
    coup_line,
    coup,
    work,
    lower_inv,
    basis_slab_t,
    mix,
    staged,
    passed,
    local_sem,
    a_local_sem,
    a_send_sem,
    a_recv_sem,
    plane_send_sem,
    plane_recv_sem,
    line_send_sem,
    line_recv_sem,
    ring_send_sem,
    ring_recv_sem,
    side_send_sem,
    side_recv_sem,
    out_send_sem,
    out_recv_sem,
    pass_send_sem,
    pass_recv_sem,
):
    r = lax.axis_index("row")
    c = lax.axis_index("col")
    z = c // 2
    core = c % 2
    plane = 2 * rows
    q = core * rows + r
    half_ring = chips // 2
    half = p_all.shape[2]
    block = 2 * half
    width = p_all.shape[3]
    steps = chips - 1

    def chip(offset):
        return (z + offset + 2 * chips) % chips

    def at_plane(index):
        return (index % rows, 2 * z + index // rows)

    def at_chip(index):
        return (r, 2 * index + core)

    right, left = at_chip(chip(1)), at_chip(chip(-1))
    sibling = (r, 2 * z + (1 - core))

    panel_load = [
        pltpu.make_async_copy(
            panel_hbm.at[pl.ds(h * half, half)], p_all.at[z, h], local_sem.at[h]
        )
        for h in range(2)
    ]
    rest_load = [
        pltpu.make_async_copy(
            rest_hbm.at[pl.ds(h * half, half)], rest.at[h], local_sem.at[2 + h]
        )
        for h in range(2)
    ]

    def block_of(i):
        magnitude = half_ring - (i + 1) // 2
        sign = 1 - 2 * ((i + 1) % 2)
        return chip(jnp.where(i == 0, half_ring, magnitude * sign))

    def a_local(i):
        target = block_of(i)
        start = pl.multiple_of((2 * target + core) * block, block)
        return pltpu.make_async_copy(
            a_hbm.at[pl.ds(start, block)], a_buf.at[core, target], a_local_sem.at[i]
        )

    def a_remote(i):
        target = block_of(i)
        start = pl.multiple_of((2 * target + 1 - core) * block, block)
        return pltpu.make_async_remote_copy(
            src_ref=a_hbm.at[pl.ds(start, block)],
            dst_ref=a_buf.at[core, target],
            send_sem=a_send_sem.at[i],
            recv_sem=a_recv_sem.at[i],
            device_id=sibling,
            device_id_type=MESH,
        )

    for copy in panel_load + rest_load:
        copy.start()

    @pl.loop(0, chips)
    def _(i):
        a_local(i).start()

    barrier = pltpu.get_barrier_semaphore()

    @pl.loop(1, plane)
    def _(i):
        pl.semaphore_signal(
            barrier, inc=1, device_id=at_plane((q + i) % plane), device_id_type=MESH
        )

    @pl.loop(1, chips)
    def _(i):
        pl.semaphore_signal(barrier, inc=1, device_id=at_chip(chip(i)), device_id_type=MESH)

    for copy in panel_load:
        copy.wait()
    pl.semaphore_wait(barrier, plane - 1 + chips - 1)

    def plane_copy(i, src, dst, slot):
        return pltpu.make_async_remote_copy(
            src_ref=src,
            dst_ref=dst,
            send_sem=plane_send_sem.at[slot],
            recv_sem=plane_recv_sem.at[slot],
            device_id=at_plane((q + i) % plane),
            device_id_type=MESH,
        )

    def side_copy(kind, direction, src, dst):
        return pltpu.make_async_remote_copy(
            src_ref=src,
            dst_ref=dst.at[q, 1 - direction],
            send_sem=side_send_sem.at[kind, direction],
            recv_sem=side_recv_sem.at[kind, direction],
            device_id=(right, left)[direction],
            device_id_type=MESH,
        )

    def plane_gather_start(src, dst, slot):
        @pl.loop(1, plane)
        def _(i):
            plane_copy(i, src, dst.at[q], slot).start()

    def plane_scatter_start(src, dst, slot):
        @pl.loop(1, plane)
        def _(i):
            plane_copy(i, src.at[(q + i) % plane], dst.at[q], slot).start()

    def plane_wait_recv(dst, slot):
        whole = dst.at[pl.ds(0, plane - 1)]
        pltpu.make_async_copy(whole, whole, plane_recv_sem.at[slot]).wait()

    def plane_wait_send(dst, slot):
        whole = dst.at[pl.ds(0, plane - 1)]
        pltpu.make_async_copy(whole, whole, plane_send_sem.at[slot]).wait()

    def line_start(buf, slot):
        @pl.loop(1, chips)
        def _(i):
            pltpu.make_async_remote_copy(
                src_ref=buf.at[z],
                dst_ref=buf.at[z],
                send_sem=line_send_sem.at[slot],
                recv_sem=line_recv_sem.at[slot],
                device_id=at_chip(chip(i)),
                device_id_type=MESH,
            ).start()

    def line_wait(buf, sem, slot):
        whole = buf.at[pl.ds(0, chips - 1)]
        pltpu.make_async_copy(whole, whole, sem.at[slot]).wait()

    def sum_first(ref, count):
        total = ref[0]
        for i in range(1, count):
            total = total + ref[i]
        return total

    def ring(kind, direction, n, src, dst):
        return pltpu.make_async_remote_copy(
            src_ref=src,
            dst_ref=dst,
            send_sem=ring_send_sem.at[kind, direction, n],
            recv_sem=ring_recv_sem.at[kind, direction, n],
            device_id=(right, left)[direction],
            device_id_type=MESH,
        )

    def gather_slot(direction, n, shift):
        away = n // 2 + shift
        h = (1 if n % 2 == 0 else 0) if direction == 0 else (0 if n % 2 == 0 else 1)
        return chip(-away if direction == 0 else away), h

    def gather_copy(buf, kind, direction, n):
        at, h = gather_slot(direction, n, 0)
        return ring(kind, direction, n, buf.at[at, h], buf.at[at, h])

    def gather_wait(buf, kind, direction, n):
        at, h = gather_slot(direction, n, 1)
        ring(kind, direction, n, buf.at[at, h], buf.at[at, h]).wait_recv()

    waited = set()

    def gather_need(buf, kind, direction, n):
        if n >= 0 and (kind, direction, n) not in waited:
            waited.add((kind, direction, n))
            gather_wait(buf, kind, direction, n)

    def gather_send(buf, kind, n):
        if n >= steps - 2:
            return
        for direction in range(2):
            if n >= 2:
                gather_need(buf, kind, direction, n - 2)
            gather_copy(buf, kind, direction, n).start()

    def sum_slot(direction, n):
        away = half_ring - (n + 1) // 2
        h = n % 2 if direction == 0 else 1 - n % 2
        return chip(away if direction == 0 else -away), h

    def sum_copy(direction, n):
        at, h = sum_slot(direction, n)
        return ring(1, direction, n, t_part.at[at, h], t_recv.at[direction, n])

    def sum_send(n):
        if n >= steps:
            return
        for direction in range(2):
            if n >= 2:
                sum_copy(direction, n - 2).wait_recv()
                at, h = sum_slot(direction, n)
                t_part[at, h] = t_part[at, h] + t_recv[direction, n - 2]
            sum_copy(direction, n).start()

    def panel_send(n):
        gather_send(p_all, 0, n)

    def image_send(n):
        gather_send(z_all, 2, n)

    for direction in range(2):
        side_copy(0, direction, p_all.at[z, 0, pl.ds(0, PIECE)], p_side).start()
    panel_send(0)

    @pl.loop(0, chips)
    def _(i):
        a_remote(i).start()

    own = p_all[z].reshape(block, width)
    gram_src[...] = dot(own, own, ((0,), (0,))).reshape(gram_src.shape)
    plane_scatter_start(gram_src, gram_recv, 1)
    gram_recv[q] = gram_src[q]
    plane_gather_start(p_all.at[z, 0, pl.ds(0, PIECE)], p_slab, 0)
    p_slab[q] = p_all[z, 0, 0:PIECE]

    def partial_sums(i):
        target = block_of(i)
        a_local(i).wait()
        pltpu.make_async_remote_copy(
            src_ref=a_buf.at[1 - core, target],
            dst_ref=a_buf.at[1 - core, target],
            send_sem=a_send_sem.at[i],
            recv_sem=a_recv_sem.at[i],
            device_id=sibling,
            device_id_type=MESH,
        ).wait_recv()
        slab = p_slab[...].reshape(plane * PIECE, width)
        both = jnp.concatenate([a_buf[0, target], a_buf[1, target]], axis=1)
        t_part[target] = dot(both, slab).reshape(2, half, width)

    plane_wait_recv(gram_recv, 1)
    gram_line[z] = sum_first(gram_recv, plane)
    line_start(gram_line, 0)
    panel_send(1)
    plane_wait_recv(p_slab, 0)
    partial_sums(0)
    sum_send(0)

    @pl.loop(1, 3)
    def _(i):
        partial_sums(i)

    sum_send(1)
    panel_send(2)
    line_wait(gram_line, line_recv_sem, 0)
    gram[q] = sum_first(gram_line, chips)
    plane_gather_start(gram.at[q], gram, 2)

    @pl.loop(3, chips)
    def _(i):
        partial_sums(i)

    nb = width // 2
    chunk = nb // 4

    def eliminate(first):
        size = nb - first
        lanes = lax.broadcasted_iota(jnp.int32, (1, nb), 1)
        sub = lax.broadcasted_iota(jnp.int32, (size, 1), 0) + first

        @pl.loop(first, first + chunk)
        def _(j):
            pivot_row = work[pl.ds(j, 1), :]
            pick = lanes == j
            pivot = jnp.sum(jnp.where(pick, pivot_row[:, :nb], 0.0), axis=1, keepdims=True)
            body = work[first:, :]
            column = jnp.sum(jnp.where(pick, body[:, :nb], 0.0), axis=1, keepdims=True)
            factor = jnp.where(sub > j, column / pivot, 0.0)
            work[first:, :] = body - factor * pivot_row

    def load_work(matrix):
        row_id = lax.broadcasted_iota(jnp.int32, (nb, nb), 0)
        col_id = lax.broadcasted_iota(jnp.int32, (nb, nb), 1)
        work[:, :nb] = matrix
        work[:, nb:] = jnp.where(row_id == col_id, 1.0, 0.0)

    def factors():
        row_id = lax.broadcasted_iota(jnp.int32, (nb, nb), 0)
        col_id = lax.broadcasted_iota(jnp.int32, (nb, nb), 1)
        upper = work[:, :nb]
        diagonal = jnp.sum(jnp.where(row_id == col_id, upper, 0.0), axis=1, keepdims=True)
        scale = 1.0 / jnp.sqrt(diagonal)
        return jnp.where(col_id >= row_id, upper * scale, 0.0), work[:, nb:] * scale

    for direction in range(2):
        side_copy(0, direction, p_all.at[z, 0, pl.ds(0, PIECE)], p_side).wait_recv()
    plane_gather_start(p_side.at[q], p_side, 6)
    plane_wait_recv(gram, 2)
    gram_rows = gram_src.shape[1]
    whole_gram = gram[...].reshape(plane * gram_rows, width)
    load_work(whole_gram[:nb, :nb])
    eliminate(0)
    eliminate(chunk)
    sum_send(2)
    eliminate(2 * chunk)
    sum_send(3)
    eliminate(3 * chunk)
    upper_a, inverse_a = factors()
    r_ref[:nb, :nb] = upper_a
    lower_inv[:nb, :nb] = inverse_a
    whole_gram = gram[...].reshape(plane * gram_rows, width)
    cross = dot(inverse_a, whole_gram[:nb, nb:])
    r_ref[:nb, nb:] = cross
    r_ref[nb:, :nb] = jnp.zeros((nb, nb), jnp.float32)
    lower_inv[:nb, nb:] = jnp.zeros((nb, nb), jnp.float32)
    load_work(whole_gram[nb:, nb:] - dot(cross, cross, ((0,), (0,))))
    eliminate(0)
    sum_send(4)
    eliminate(chunk)
    sum_send(5)
    eliminate(2 * chunk)
    sum_send(6)
    panel_send(3)
    panel_send(4)
    eliminate(3 * chunk)
    upper_b, inverse_b = factors()
    r_ref[nb:, nb:] = upper_b
    lower_inv[nb:, nb:] = inverse_b
    lower_inv[nb:, :nb] = -dot(inverse_b, dot(r_ref[:nb, nb:], lower_inv[:nb, :nb], ((0,), (0,))))

    slab = plane * PIECE
    inverse = lower_inv[...]
    plane_wait_recv(p_side, 6)

    def columns_of(i):
        return slice(i * slab, (i + 1) * slab)

    def three(own_rows, side):
        return (
            own_rows[...].reshape(slab, width),
            side[:, 0].reshape(slab, width),
            side[:, 1].reshape(slab, width),
        )

    for i, slab_rows in enumerate(three(p_slab, p_side)):
        basis_slab_t[:, columns_of(i)] = dot(inverse, slab_rows, ((1,), (1,)))
    own_basis = dot(p_all[z].reshape(block, width), inverse, ((1,), (1,)))

    for copy in rest_load:
        copy.wait()
    for direction in range(2):
        for n in (steps - 2, steps - 1):
            sum_copy(direction, n).wait_recv()
    for h in range(2):
        first = t_recv[0, steps - 2 if h == 1 else steps - 1]
        second = t_recv[1, steps - 2 if h == 0 else steps - 1]
        total = t_part[z, h] + first + second
        z_all[z, h] = rest[h] + 2.0 * dot(total, inverse, ((1,), (1,)))
    for direction in range(2):
        side_copy(1, direction, z_all.at[z, 0, pl.ds(0, PIECE)], z_side).start()
    image_send(0)
    coup_src[...] = dot(
        own_basis, z_all[z].reshape(block, width), ((0,), (0,))
    ).reshape(coup_src.shape)
    plane_scatter_start(coup_src, coup_recv, 4)
    coup_recv[q] = coup_src[q]
    plane_gather_start(z_all.at[z, 0, pl.ds(0, PIECE)], z_slab, 3)
    z_slab[q] = z_all[z, 0, 0:PIECE]
    plane_wait_recv(coup_recv, 4)
    coup_line[z] = sum_first(coup_recv, plane)
    line_start(coup_line, 1)
    image_send(1)
    for direction in range(2):
        side_copy(1, direction, z_all.at[z, 0, pl.ds(0, PIECE)], z_side).wait_recv()
    plane_gather_start(z_side.at[q], z_side, 7)
    image_send(2)
    line_wait(coup_line, line_recv_sem, 1)
    coup[q] = sum_first(coup_line, chips)
    plane_gather_start(coup.at[q], coup, 5)
    image_send(3)
    plane_wait_recv(z_slab, 3)
    plane_wait_recv(z_side, 7)
    plane_wait_recv(coup, 5)
    coupling = coup[...].reshape(width, width)
    for i, slab_rows in enumerate(three(z_slab, z_side)):
        slab_t = basis_slab_t[:, columns_of(i)]
        inner = jnp.transpose(slab_rows)
        inner = inner - dot(coupling, slab_t) - dot(coupling, slab_t, ((0,), (0,)))
        mix[:, columns_of(i)] = dot(lower_inv[...], inner, ((0,), (0,)))

    columns = slab // 2

    def first_row(at, core_of_rows, h):
        return pl.multiple_of((2 * at + core_of_rows) * block + h * half, half)

    def update_block(at, h, i):
        value = dot(p_all[at, h], mix[:, columns_of(i)])
        value = value + dot(z_all[at, h], basis_slab_t[:, columns_of(i)])
        return value[:, :columns], value[:, columns:]

    def swap_copy(slot, start):
        return pltpu.make_async_remote_copy(
            src_ref=staged.at[slot],
            dst_ref=out_ref.at[pl.ds(start, half)],
            send_sem=out_send_sem.at[slot],
            recv_sem=out_recv_sem.at[slot],
            device_id=sibling,
            device_id_type=MESH,
        )

    done = []

    def update(at, h):
        slot = len(done)
        low, high = update_block(at, h, 0)
        staged[slot] = jnp.where(core == 0, high, low)
        start = first_row(at, core, h)
        swap_copy(slot, start).start()
        out_ref[pl.ds(start, half), :] = jnp.where(core == 0, low, high)
        done.append((at, h))

    def pass_copy(direction, n, source, target, at, h):
        return pltpu.make_async_remote_copy(
            src_ref=passed.at[direction, n, target],
            dst_ref=out_ref.at[pl.ds(first_row(at, source, h), half)],
            send_sem=pass_send_sem.at[direction, n, target],
            recv_sem=pass_recv_sem.at[direction, n, source],
            device_id=(r, 2 * chip(1 if direction == 0 else -1) + target),
            device_id_type=MESH,
        )

    def pass_send(n):
        for direction in range(2):
            last = steps - 2 + n
            gather_need(z_all, 2, direction, last - 2)
            gather_need(p_all, 0, direction, last - 2)
            at, h = gather_slot(direction, last, 0)
            low, high = update_block(at, h, 1 + direction)
            passed[direction, n, 0] = low
            passed[direction, n, 1] = high
            for target in range(2):
                pass_copy(direction, n, core, target, at, h).start()

    def update_received(n):
        for direction in range(2):
            gather_need(z_all, 2, direction, n)
            gather_need(p_all, 0, direction, n)
            update(*gather_slot(direction, n, 1))

    update(z, 0)
    update(z, 1)
    for n in range(steps - 4):
        if n == 1:
            image_send(4)
        update_received(n)
    pass_send(0)
    pass_send(1)
    for n in range(max(steps - 4, 0), steps - 2):
        update_received(n)

    for slot, (at, h) in enumerate(done):
        swap_copy(slot, first_row(at, core, h)).wait_send()
        swap_copy(slot, first_row(at, 1 - core, h)).wait_recv()
    for n in range(2):
        for direction in range(2):
            last = steps - 2 + n
            for index in range(2):
                at, h = gather_slot(direction, last, 0)
                pass_copy(direction, n, core, index, at, h).wait_send()
                at, h = gather_slot(direction, last, 1)
                pass_copy(direction, n, index, index, at, h).wait_recv()

    for direction in range(2):
        for n in range(steps):
            sum_copy(direction, n).wait_send()
        for n in range(steps - 2):
            gather_copy(p_all, 0, direction, n).wait_send()
            gather_copy(z_all, 2, direction, n).wait_send()
        side_copy(0, direction, p_all.at[z, 0, pl.ds(0, PIECE)], p_side).wait_send()
        side_copy(1, direction, z_all.at[z, 0, pl.ds(0, PIECE)], z_side).wait_send()

    @pl.loop(0, chips)
    def _(i):
        a_remote(i).wait_send()

    plane_wait_send(p_slab, 0)
    plane_wait_send(gram_recv, 1)
    plane_wait_send(gram, 2)
    plane_wait_send(z_slab, 3)
    plane_wait_send(coup_recv, 4)
    plane_wait_send(coup, 5)
    plane_wait_send(p_side, 6)
    plane_wait_send(z_side, 7)
    line_wait(gram_line, line_send_sem, 0)
    line_wait(coup_line, line_send_sem, 1)


def per_device(panel, image_rest, a_slab):
    f32 = jnp.float32
    rows = lax.axis_size("row")
    chips = lax.axis_size("col") // 2
    block, width = panel.shape
    columns = a_slab.shape[1]
    half = block // 2
    plane = 2 * rows
    gram_rows = width // plane
    slab = plane * PIECE
    steps = chips - 1
    dma = pltpu.SemaphoreType.DMA
    hbm = pl.BlockSpec(memory_space=pltpu.HBM)
    vmem = pl.BlockSpec(memory_space=pltpu.VMEM)
    reduction = [
        pltpu.VMEM((plane, gram_rows, width), f32),
        pltpu.VMEM((plane, gram_rows, width), f32),
        pltpu.VMEM((chips, gram_rows, width), f32),
        pltpu.VMEM((plane, gram_rows, width), f32),
    ]
    return pl.pallas_call(
        functools.partial(kernel, rows, chips),
        out_shape=(
            pltpu.VMEM((width, width), f32),
            pltpu.VMEM(a_slab.shape, f32),
        ),
        in_specs=[hbm, hbm, hbm],
        out_specs=(vmem, vmem),
        scratch_shapes=[
            pltpu.VMEM((2, chips, block, columns), f32),
            pltpu.VMEM((chips, 2, half, width), f32),
            pltpu.VMEM((chips, 2, half, width), f32),
            pltpu.VMEM((chips, 2, half, width), f32),
            pltpu.VMEM((2, steps, half, width), f32),
            pltpu.VMEM((2, half, width), f32),
            pltpu.VMEM((plane, PIECE, width), f32),
            pltpu.VMEM((plane, PIECE, width), f32),
            pltpu.VMEM((plane, 2, PIECE, width), f32),
            pltpu.VMEM((plane, 2, PIECE, width), f32),
            *reduction,
            *reduction,
            pltpu.VMEM((width // 2, width), f32),
            pltpu.VMEM((width, width), f32),
            pltpu.VMEM((width, 3 * slab), f32),
            pltpu.VMEM((width, 3 * slab), f32),
            pltpu.VMEM((2 * chips - 4, half, columns), f32),
            pltpu.VMEM((2, 2, 2, half, columns), f32),
            dma((4,)),
            dma((chips,)),
            dma((chips,)),
            dma((chips,)),
            dma((8,)),
            dma((8,)),
            dma((2,)),
            dma((2,)),
            dma((3, 2, steps)),
            dma((3, 2, steps)),
            dma((2, 2)),
            dma((2, 2)),
            dma((2 * chips - 4,)),
            dma((2 * chips - 4,)),
            dma((2, 2, 2)),
            dma((2, 2, 2)),
        ],
        compiler_params=pltpu.CompilerParams(
            collective_id=0, has_side_effects=True, vmem_limit_bytes=56 * 1024 * 1024
        ),
    )(panel, image_rest, a_slab)


def solution(mesh):
    placed = (P(("row", "col"), None), P(("row", "col"), None), P("row", "col"))
    return jax.shard_map(
        per_device, mesh=mesh, in_specs=placed, out_specs=(P(), P("row", "col")), check_vma=False
    )
```

```python
import functools

import jax
import jax.numpy as jnp
from jax import lax
from jax.experimental import pallas as pl
from jax.experimental.pallas import tpu as pltpu
from jax.sharding import PartitionSpec as P

MESH = pl.DeviceIdType.MESH
HIGHEST = lax.Precision.HIGHEST
PIECE = 8


def dot(left, right, contract=((1,), (0,))):
    return lax.dot_general(
        left, right, (contract, ((), ())), precision=HIGHEST, preferred_element_type=jnp.float32
    )


def kernel(
    rows,
    chips,
    panel_hbm,
    rest_hbm,
    a_hbm,
    r_ref,
    out_ref,
    a_buf,
    p_all,
    z_all,
    t_part,
    t_recv,
    rest,
    p_slab,
    z_slab,
    p_side,
    z_side,
    gram_src,
    gram_recv,
    gram_line,
    gram,
    coup_src,
    coup_recv,
    coup_piece,
    coup,
    work,
    lower_inv,
    basis_slab_t,
    mix,
    staged,
    passed,
    local_sem,
    a_local_sem,
    a_send_sem,
    a_recv_sem,
    plane_send_sem,
    plane_recv_sem,
    line_send_sem,
    line_recv_sem,
    ring_send_sem,
    ring_recv_sem,
    side_send_sem,
    side_recv_sem,
    out_send_sem,
    out_recv_sem,
    pass_send_sem,
    pass_recv_sem,
):
    r = lax.axis_index("row")
    c = lax.axis_index("col")
    z = c // 2
    core = c % 2
    plane = 2 * rows
    q = core * rows + r
    half_ring = chips // 2
    half = p_all.shape[2]
    block = 2 * half
    width = p_all.shape[3]
    steps = chips - 1

    def chip(offset):
        return (z + offset + 2 * chips) % chips

    def at_plane(index):
        return (index % rows, 2 * z + index // rows)

    def at_chip(index):
        return (r, 2 * index + core)

    right, left = at_chip(chip(1)), at_chip(chip(-1))
    sibling = (r, 2 * z + (1 - core))

    panel_load = [
        pltpu.make_async_copy(
            panel_hbm.at[pl.ds(h * half, half)], p_all.at[z, h], local_sem.at[h]
        )
        for h in range(2)
    ]
    rest_load = [
        pltpu.make_async_copy(
            rest_hbm.at[pl.ds(h * half, half)], rest.at[h], local_sem.at[2 + h]
        )
        for h in range(2)
    ]

    def block_of(i):
        magnitude = half_ring - (i + 1) // 2
        sign = 1 - 2 * ((i + 1) % 2)
        return chip(jnp.where(i == 0, half_ring, magnitude * sign))

    def a_local(i):
        target = block_of(i)
        start = pl.multiple_of((2 * target + core) * block, block)
        return pltpu.make_async_copy(
            a_hbm.at[pl.ds(start, block)], a_buf.at[core, target], a_local_sem.at[i]
        )

    def a_remote(i):
        target = block_of(i)
        start = pl.multiple_of((2 * target + 1 - core) * block, block)
        return pltpu.make_async_remote_copy(
            src_ref=a_hbm.at[pl.ds(start, block)],
            dst_ref=a_buf.at[core, target],
            send_sem=a_send_sem.at[i],
            recv_sem=a_recv_sem.at[i],
            device_id=sibling,
            device_id_type=MESH,
        )

    for copy in panel_load:
        copy.start()

    barrier = pltpu.get_barrier_semaphore()

    @pl.loop(1, plane)
    def _(i):
        pl.semaphore_signal(
            barrier, inc=1, device_id=at_plane((q + i) % plane), device_id_type=MESH
        )

    @pl.loop(1, chips)
    def _(i):
        pl.semaphore_signal(barrier, inc=1, device_id=at_chip(chip(i)), device_id_type=MESH)

    for copy in rest_load:
        copy.start()

    @pl.loop(0, chips)
    def _(i):
        a_local(i).start()

    for copy in panel_load:
        copy.wait()
    pl.semaphore_wait(barrier, plane - 1 + chips - 1)

    def plane_copy(i, src, dst, slot):
        return pltpu.make_async_remote_copy(
            src_ref=src,
            dst_ref=dst,
            send_sem=plane_send_sem.at[slot],
            recv_sem=plane_recv_sem.at[slot],
            device_id=at_plane((q + i) % plane),
            device_id_type=MESH,
        )

    def side_copy(kind, direction, src, dst):
        return pltpu.make_async_remote_copy(
            src_ref=src,
            dst_ref=dst.at[q, 1 - direction],
            send_sem=side_send_sem.at[kind, direction],
            recv_sem=side_recv_sem.at[kind, direction],
            device_id=(right, left)[direction],
            device_id_type=MESH,
        )

    def plane_gather_start(src, dst, slot):
        @pl.loop(1, plane)
        def _(i):
            plane_copy(i, src, dst.at[q], slot).start()

    def plane_scatter_start(src, dst, slot):
        @pl.loop(1, plane)
        def _(i):
            plane_copy(i, src.at[(q + i) % plane], dst.at[q], slot).start()

    def plane_wait_recv(dst, slot):
        whole = dst.at[pl.ds(0, plane - 1)]
        pltpu.make_async_copy(whole, whole, plane_recv_sem.at[slot]).wait()

    def plane_wait_send(dst, slot):
        whole = dst.at[pl.ds(0, plane - 1)]
        pltpu.make_async_copy(whole, whole, plane_send_sem.at[slot]).wait()

    def line_copy(i, src, dst, slot):
        return pltpu.make_async_remote_copy(
            src_ref=src,
            dst_ref=dst,
            send_sem=line_send_sem.at[slot],
            recv_sem=line_recv_sem.at[slot],
            device_id=at_chip(chip(i)),
            device_id_type=MESH,
        )

    def line_scatter(total, src, dst, slot):
        share = src.shape[1]
        for i in range(chips):
            src[i] = total[i * share : (i + 1) * share]

        @pl.loop(1, chips)
        def _(i):
            line_copy(i, src.at[chip(i)], dst.at[z], slot).start()

        dst[z] = src[z]

    def line_gather(received, dst, slot):
        line_wait(received, line_recv_sem, slot)
        dst[z] = sum_first(received, chips)

        @pl.loop(1, chips)
        def _(i):
            line_copy(i, dst.at[z], dst.at[z], slot + 1).start()

    def line_finish(gathered, dst, slot):
        line_wait(gathered, line_recv_sem, slot + 1)
        share = gathered.shape[1]
        for i in range(chips):
            dst[q, i * share : (i + 1) * share] = gathered[i]

    def line_wait(buf, sem, slot):
        whole = buf.at[pl.ds(0, chips - 1)]
        pltpu.make_async_copy(whole, whole, sem.at[slot]).wait()

    def sum_first(ref, count):
        total = ref[0]
        for i in range(1, count):
            total = total + ref[i]
        return total

    def ring(kind, direction, n, src, dst):
        return pltpu.make_async_remote_copy(
            src_ref=src,
            dst_ref=dst,
            send_sem=ring_send_sem.at[kind, direction, n],
            recv_sem=ring_recv_sem.at[kind, direction, n],
            device_id=(right, left)[direction],
            device_id_type=MESH,
        )

    def gather_slot(direction, n, shift):
        away = n // 2 + shift
        h = (1 if n % 2 == 0 else 0) if direction == 0 else (0 if n % 2 == 0 else 1)
        return chip(-away if direction == 0 else away), h

    def gather_copy(buf, kind, direction, n):
        at, h = gather_slot(direction, n, 0)
        return ring(kind, direction, n, buf.at[at, h], buf.at[at, h])

    def gather_wait(buf, kind, direction, n):
        at, h = gather_slot(direction, n, 1)
        ring(kind, direction, n, buf.at[at, h], buf.at[at, h]).wait_recv()

    waited = set()

    def gather_need(buf, kind, direction, n):
        if n >= 0 and (kind, direction, n) not in waited:
            waited.add((kind, direction, n))
            gather_wait(buf, kind, direction, n)

    def gather_send(buf, kind, n):
        if n >= steps - 2:
            return
        for direction in range(2):
            if n >= 2:
                gather_need(buf, kind, direction, n - 2)
            gather_copy(buf, kind, direction, n).start()

    def sum_slot(direction, n):
        away = half_ring - (n + 1) // 2
        h = n % 2 if direction == 0 else 1 - n % 2
        return chip(away if direction == 0 else -away), h

    def sum_copy(direction, n):
        at, h = sum_slot(direction, n)
        return ring(1, direction, n, t_part.at[at, h], t_recv.at[direction, n])

    def sum_send(n):
        if n >= steps:
            return
        for direction in range(2):
            if n >= 2:
                sum_copy(direction, n - 2).wait_recv()
                at, h = sum_slot(direction, n)
                t_part[at, h] = t_part[at, h] + t_recv[direction, n - 2]
            sum_copy(direction, n).start()

    def panel_send(n):
        gather_send(p_all, 0, n)

    def image_send(n):
        gather_send(z_all, 2, n)

    for direction in range(2):
        side_copy(0, direction, p_all.at[z, 0, pl.ds(0, PIECE)], p_side).start()
    panel_send(0)

    @pl.loop(0, chips)
    def _(i):
        a_remote(i).start()

    own = p_all[z].reshape(block, width)
    gram_src[...] = dot(own, own, ((0,), (0,))).reshape(gram_src.shape)
    plane_scatter_start(gram_src, gram_recv, 1)
    gram_recv[q] = gram_src[q]
    plane_gather_start(p_all.at[z, 0, pl.ds(0, PIECE)], p_slab, 0)
    p_slab[q] = p_all[z, 0, 0:PIECE]

    def partial_sums(i):
        target = block_of(i)
        a_local(i).wait()
        pltpu.make_async_remote_copy(
            src_ref=a_buf.at[1 - core, target],
            dst_ref=a_buf.at[1 - core, target],
            send_sem=a_send_sem.at[i],
            recv_sem=a_recv_sem.at[i],
            device_id=sibling,
            device_id_type=MESH,
        ).wait_recv()
        slab = p_slab[...].reshape(plane * PIECE, width)
        both = jnp.concatenate([a_buf[0, target], a_buf[1, target]], axis=1)
        t_part[target] = dot(both, slab).reshape(2, half, width)

    plane_wait_recv(gram_recv, 1)
    line_scatter(sum_first(gram_recv, plane), gram_line.at[0], gram_line.at[1], 0)
    panel_send(1)
    plane_wait_recv(p_slab, 0)
    partial_sums(0)
    line_gather(gram_line.at[1], gram_line.at[2], 0)
    sum_send(0)

    @pl.loop(1, 3)
    def _(i):
        partial_sums(i)

    sum_send(1)
    panel_send(2)
    line_finish(gram_line.at[2], gram, 0)
    plane_gather_start(gram.at[q], gram, 2)

    @pl.loop(3, chips)
    def _(i):
        partial_sums(i)

    nb = width // 2
    chunk = nb // 4

    def eliminate(first):
        size = nb - first
        lanes = lax.broadcasted_iota(jnp.int32, (1, nb), 1)
        sub = lax.broadcasted_iota(jnp.int32, (size, 1), 0) + first

        @pl.loop(first, first + chunk)
        def _(j):
            pivot_row = work[pl.ds(j, 1), :]
            pick = lanes == j
            pivot = jnp.sum(jnp.where(pick, pivot_row[:, :nb], 0.0), axis=1, keepdims=True)
            body = work[first:, :]
            column = jnp.sum(jnp.where(pick, body[:, :nb], 0.0), axis=1, keepdims=True)
            factor = jnp.where(sub > j, column / pivot, 0.0)
            work[first:, :] = body - factor * pivot_row

    def load_work(matrix):
        row_id = lax.broadcasted_iota(jnp.int32, (nb, nb), 0)
        col_id = lax.broadcasted_iota(jnp.int32, (nb, nb), 1)
        work[:, :nb] = matrix
        work[:, nb:] = jnp.where(row_id == col_id, 1.0, 0.0)

    def factors():
        row_id = lax.broadcasted_iota(jnp.int32, (nb, nb), 0)
        col_id = lax.broadcasted_iota(jnp.int32, (nb, nb), 1)
        upper = work[:, :nb]
        diagonal = jnp.sum(jnp.where(row_id == col_id, upper, 0.0), axis=1, keepdims=True)
        scale = 1.0 / jnp.sqrt(diagonal)
        return jnp.where(col_id >= row_id, upper * scale, 0.0), work[:, nb:] * scale

    for direction in range(2):
        side_copy(0, direction, p_all.at[z, 0, pl.ds(0, PIECE)], p_side).wait_recv()
    plane_gather_start(p_side.at[q], p_side, 6)
    plane_wait_recv(gram, 2)
    gram_rows = gram_src.shape[1]
    whole_gram = gram[...].reshape(plane * gram_rows, width)
    load_work(whole_gram[:nb, :nb])
    eliminate(0)
    eliminate(chunk)
    sum_send(2)
    eliminate(2 * chunk)
    sum_send(3)
    eliminate(3 * chunk)
    upper_a, inverse_a = factors()
    r_ref[:nb, :nb] = upper_a
    lower_inv[:nb, :nb] = inverse_a
    whole_gram = gram[...].reshape(plane * gram_rows, width)
    cross = dot(inverse_a, whole_gram[:nb, nb:])
    r_ref[:nb, nb:] = cross
    r_ref[nb:, :nb] = jnp.zeros((nb, nb), jnp.float32)
    lower_inv[:nb, nb:] = jnp.zeros((nb, nb), jnp.float32)
    load_work(whole_gram[nb:, nb:] - dot(cross, cross, ((0,), (0,))))
    eliminate(0)
    sum_send(4)
    eliminate(chunk)
    sum_send(5)
    eliminate(2 * chunk)
    sum_send(6)
    panel_send(3)
    panel_send(4)
    eliminate(3 * chunk)
    upper_b, inverse_b = factors()
    r_ref[nb:, nb:] = upper_b
    lower_inv[nb:, nb:] = inverse_b
    lower_inv[nb:, :nb] = -dot(inverse_b, dot(r_ref[:nb, nb:], lower_inv[:nb, :nb], ((0,), (0,))))

    slab = plane * PIECE
    inverse = lower_inv[...]
    plane_wait_recv(p_side, 6)

    def columns_of(i):
        return slice(i * slab, (i + 1) * slab)

    def three(own_rows, side):
        return (
            own_rows[...].reshape(slab, width),
            side[:, 0].reshape(slab, width),
            side[:, 1].reshape(slab, width),
        )

    for i, slab_rows in enumerate(three(p_slab, p_side)):
        basis_slab_t[:, columns_of(i)] = dot(inverse, slab_rows, ((1,), (1,)))
    own_basis = dot(p_all[z].reshape(block, width), inverse, ((1,), (1,)))

    for copy in rest_load:
        copy.wait()
    for direction in range(2):
        for n in (steps - 2, steps - 1):
            sum_copy(direction, n).wait_recv()
    for h in range(2):
        first = t_recv[0, steps - 2 if h == 1 else steps - 1]
        second = t_recv[1, steps - 2 if h == 0 else steps - 1]
        total = t_part[z, h] + first + second
        z_all[z, h] = rest[h] + 2.0 * dot(total, inverse, ((1,), (1,)))
    for direction in range(2):
        side_copy(1, direction, z_all.at[z, 0, pl.ds(0, PIECE)], z_side).start()
    image_send(0)
    coup_src[...] = dot(
        own_basis, z_all[z].reshape(block, width), ((0,), (0,))
    ).reshape(coup_src.shape)
    plane_scatter_start(coup_src, coup_recv, 4)
    coup_recv[q] = coup_src[q]
    plane_gather_start(z_all.at[z, 0, pl.ds(0, PIECE)], z_slab, 3)
    z_slab[q] = z_all[z, 0, 0:PIECE]
    plane_wait_recv(coup_recv, 4)
    coup_piece[z] = sum_first(coup_recv, plane)

    @pl.loop(1, chips)
    def _(i):
        line_copy(i, coup_piece.at[z], coup_piece.at[z], 2).start()

    image_send(1)
    for direction in range(2):
        side_copy(1, direction, z_all.at[z, 0, pl.ds(0, PIECE)], z_side).wait_recv()
    plane_gather_start(z_side.at[q], z_side, 7)
    image_send(2)
    line_wait(coup_piece, line_recv_sem, 2)
    coup[q] = sum_first(coup_piece, chips)
    plane_gather_start(coup.at[q], coup, 5)
    image_send(3)
    plane_wait_recv(z_slab, 3)
    plane_wait_recv(z_side, 7)
    plane_wait_recv(coup, 5)
    coupling = coup[...].reshape(width, width)
    for i, slab_rows in enumerate(three(z_slab, z_side)):
        slab_t = basis_slab_t[:, columns_of(i)]
        inner = jnp.transpose(slab_rows)
        inner = inner - dot(coupling, slab_t) - dot(coupling, slab_t, ((0,), (0,)))
        mix[:, columns_of(i)] = dot(lower_inv[...], inner, ((0,), (0,)))

    columns = slab // 2

    def first_row(at, core_of_rows, h):
        return pl.multiple_of((2 * at + core_of_rows) * block + h * half, half)

    def update_block(at, h, i):
        value = dot(p_all[at, h], mix[:, columns_of(i)])
        value = value + dot(z_all[at, h], basis_slab_t[:, columns_of(i)])
        return value[:, :columns], value[:, columns:]

    def swap_copy(slot, start):
        return pltpu.make_async_remote_copy(
            src_ref=staged.at[slot],
            dst_ref=out_ref.at[pl.ds(start, half)],
            send_sem=out_send_sem.at[slot],
            recv_sem=out_recv_sem.at[slot],
            device_id=sibling,
            device_id_type=MESH,
        )

    done = []

    def update(at, h):
        slot = len(done)
        low, high = update_block(at, h, 0)
        staged[slot] = jnp.where(core == 0, high, low)
        start = first_row(at, core, h)
        swap_copy(slot, start).start()
        out_ref[pl.ds(start, half), :] = jnp.where(core == 0, low, high)
        done.append((at, h))

    def pass_copy(direction, n, source, target, at, h):
        return pltpu.make_async_remote_copy(
            src_ref=passed.at[direction, n, target],
            dst_ref=out_ref.at[pl.ds(first_row(at, source, h), half)],
            send_sem=pass_send_sem.at[direction, n, target],
            recv_sem=pass_recv_sem.at[direction, n, source],
            device_id=(r, 2 * chip(1 if direction == 0 else -1) + target),
            device_id_type=MESH,
        )

    def pass_send(n):
        for direction in range(2):
            last = steps - 2 + n
            gather_need(z_all, 2, direction, last - 2)
            gather_need(p_all, 0, direction, last - 2)
            at, h = gather_slot(direction, last, 0)
            low, high = update_block(at, h, 1 + direction)
            passed[direction, n, 0] = low
            passed[direction, n, 1] = high
            for target in range(2):
                pass_copy(direction, n, core, target, at, h).start()

    def update_received(n):
        for direction in range(2):
            gather_need(z_all, 2, direction, n)
            gather_need(p_all, 0, direction, n)
            update(*gather_slot(direction, n, 1))

    update(z, 0)
    update(z, 1)
    update_received(0)
    image_send(4)
    pass_send(0)
    if steps > 4:
        update_received(1)
    pass_send(1)
    for n in range(2, steps - 2):
        update_received(n)

    for direction in range(2):
        for n in range(steps):
            sum_copy(direction, n).wait_send()
        for n in range(steps - 2):
            gather_copy(p_all, 0, direction, n).wait_send()
            gather_copy(z_all, 2, direction, n).wait_send()
        side_copy(0, direction, p_all.at[z, 0, pl.ds(0, PIECE)], p_side).wait_send()
        side_copy(1, direction, z_all.at[z, 0, pl.ds(0, PIECE)], z_side).wait_send()

    @pl.loop(0, chips)
    def _(i):
        a_remote(i).wait_send()

    plane_wait_send(p_slab, 0)
    plane_wait_send(gram_recv, 1)
    plane_wait_send(gram, 2)
    plane_wait_send(z_slab, 3)
    plane_wait_send(coup_recv, 4)
    plane_wait_send(coup, 5)
    plane_wait_send(p_side, 6)
    plane_wait_send(z_side, 7)
    for slot in range(2):
        line_wait(gram_line.at[1], line_send_sem, slot)
    line_wait(coup_piece, line_send_sem, 2)

    for slot, (at, h) in enumerate(done):
        swap_copy(slot, first_row(at, core, h)).wait_send()
        swap_copy(slot, first_row(at, 1 - core, h)).wait_recv()
    for n in range(2):
        for direction in range(2):
            last = steps - 2 + n
            for index in range(2):
                at, h = gather_slot(direction, last, 0)
                pass_copy(direction, n, core, index, at, h).wait_send()
                at, h = gather_slot(direction, last, 1)
                pass_copy(direction, n, index, index, at, h).wait_recv()


def per_device(panel, image_rest, a_slab):
    f32 = jnp.float32
    rows = lax.axis_size("row")
    chips = lax.axis_size("col") // 2
    block, width = panel.shape
    columns = a_slab.shape[1]
    half = block // 2
    plane = 2 * rows
    gram_rows = width // plane
    slab = plane * PIECE
    steps = chips - 1
    dma = pltpu.SemaphoreType.DMA
    hbm = pl.BlockSpec(memory_space=pltpu.HBM)
    vmem = pl.BlockSpec(memory_space=pltpu.VMEM)
    piece = pltpu.VMEM((plane, gram_rows, width), f32)
    gram_line = pltpu.VMEM((3, chips, gram_rows // chips, width), f32)
    coup_piece = pltpu.VMEM((chips, gram_rows, width), f32)
    return pl.pallas_call(
        functools.partial(kernel, rows, chips),
        out_shape=(
            pltpu.VMEM((width, width), f32),
            pltpu.VMEM(a_slab.shape, f32),
        ),
        in_specs=[hbm, hbm, hbm],
        out_specs=(vmem, vmem),
        scratch_shapes=[
            pltpu.VMEM((2, chips, block, columns), f32),
            pltpu.VMEM((chips, 2, half, width), f32),
            pltpu.VMEM((chips, 2, half, width), f32),
            pltpu.VMEM((chips, 2, half, width), f32),
            pltpu.VMEM((2, steps, half, width), f32),
            pltpu.VMEM((2, half, width), f32),
            pltpu.VMEM((plane, PIECE, width), f32),
            pltpu.VMEM((plane, PIECE, width), f32),
            pltpu.VMEM((plane, 2, PIECE, width), f32),
            pltpu.VMEM((plane, 2, PIECE, width), f32),
            piece,
            piece,
            gram_line,
            piece,
            piece,
            piece,
            coup_piece,
            piece,
            pltpu.VMEM((width // 2, width), f32),
            pltpu.VMEM((width, width), f32),
            pltpu.VMEM((width, 3 * slab), f32),
            pltpu.VMEM((width, 3 * slab), f32),
            pltpu.VMEM((2 * chips - 4, half, columns), f32),
            pltpu.VMEM((2, 2, 2, half, columns), f32),
            dma((4,)),
            dma((chips,)),
            dma((chips,)),
            dma((chips,)),
            dma((8,)),
            dma((8,)),
            dma((4,)),
            dma((4,)),
            dma((3, 2, steps)),
            dma((3, 2, steps)),
            dma((2, 2)),
            dma((2, 2)),
            dma((2 * chips - 4,)),
            dma((2 * chips - 4,)),
            dma((2, 2, 2)),
            dma((2, 2, 2)),
        ],
        compiler_params=pltpu.CompilerParams(
            collective_id=0, has_side_effects=True, vmem_limit_bytes=56 * 1024 * 1024
        ),
    )(panel, image_rest, a_slab)


def solution(mesh):
    placed = (P(("row", "col"), None), P(("row", "col"), None), P("row", "col"))
    return jax.shard_map(
        per_device, mesh=mesh, in_specs=placed, out_specs=(P(), P("row", "col")), check_vma=False
    )
```

```python
import functools

import jax
import jax.numpy as jnp
from jax import lax
from jax.experimental import pallas as pl
from jax.experimental.pallas import tpu as pltpu
from jax.sharding import PartitionSpec as P

MESH = pl.DeviceIdType.MESH
HIGHEST = lax.Precision.HIGHEST
PIECE = 8


def dot(left, right, contract=((1,), (0,))):
    return lax.dot_general(
        left, right, (contract, ((), ())), precision=HIGHEST, preferred_element_type=jnp.float32
    )


def kernel(
    rows,
    chips,
    panel_hbm,
    rest_hbm,
    a_hbm,
    r_ref,
    out_ref,
    a_buf,
    p_all,
    z_all,
    t_part,
    t_recv,
    rest,
    p_slab,
    z_slab,
    p_side,
    z_side,
    gram_src,
    gram_recv,
    gram_line,
    gram,
    coup_src,
    coup_recv,
    coup_piece,
    coup,
    work,
    lower_inv,
    basis_slab_t,
    mix,
    staged,
    passed,
    local_sem,
    a_local_sem,
    a_send_sem,
    a_recv_sem,
    plane_send_sem,
    plane_recv_sem,
    line_send_sem,
    line_recv_sem,
    ring_send_sem,
    ring_recv_sem,
    side_send_sem,
    side_recv_sem,
    out_send_sem,
    out_recv_sem,
    pass_send_sem,
    pass_recv_sem,
):
    r = lax.axis_index("row")
    c = lax.axis_index("col")
    z = c // 2
    core = c % 2
    plane = 2 * rows
    q = core * rows + r
    half_ring = chips // 2
    half = p_all.shape[2]
    block = 2 * half
    width = p_all.shape[3]
    steps = chips - 1

    def chip(offset):
        return (z + offset + 2 * chips) % chips

    def at_plane(index):
        return (index % rows, 2 * z + index // rows)

    def at_chip(index):
        return (r, 2 * index + core)

    right, left = at_chip(chip(1)), at_chip(chip(-1))
    sibling = (r, 2 * z + (1 - core))

    panel_load = [
        pltpu.make_async_copy(
            panel_hbm.at[pl.ds(h * half, half)], p_all.at[z, h], local_sem.at[h]
        )
        for h in range(2)
    ]
    rest_load = [
        pltpu.make_async_copy(
            rest_hbm.at[pl.ds(h * half, half)], rest.at[h], local_sem.at[2 + h]
        )
        for h in range(2)
    ]

    def block_of(i):
        magnitude = half_ring - (i + 1) // 2
        sign = 1 - 2 * ((i + 1) % 2)
        return chip(jnp.where(i == 0, half_ring, magnitude * sign))

    def a_local(i):
        target = block_of(i)
        start = pl.multiple_of((2 * target + core) * block, block)
        return pltpu.make_async_copy(
            a_hbm.at[pl.ds(start, block)], a_buf.at[core, target], a_local_sem.at[i]
        )

    def a_remote(i):
        target = block_of(i)
        start = pl.multiple_of((2 * target + 1 - core) * block, block)
        return pltpu.make_async_remote_copy(
            src_ref=a_hbm.at[pl.ds(start, block)],
            dst_ref=a_buf.at[core, target],
            send_sem=a_send_sem.at[i],
            recv_sem=a_recv_sem.at[i],
            device_id=sibling,
            device_id_type=MESH,
        )

    for copy in panel_load:
        copy.start()

    barrier = pltpu.get_barrier_semaphore()

    @pl.loop(1, plane)
    def _(i):
        pl.semaphore_signal(
            barrier, inc=1, device_id=at_plane((q + i) % plane), device_id_type=MESH
        )

    @pl.loop(1, chips)
    def _(i):
        pl.semaphore_signal(barrier, inc=1, device_id=at_chip(chip(i)), device_id_type=MESH)

    for copy in rest_load:
        copy.start()

    @pl.loop(0, chips)
    def _(i):
        a_local(i).start()

    for copy in panel_load:
        copy.wait()
    pl.semaphore_wait(barrier, plane - 1 + chips - 1)

    def plane_copy(i, src, dst, slot):
        return pltpu.make_async_remote_copy(
            src_ref=src,
            dst_ref=dst,
            send_sem=plane_send_sem.at[slot],
            recv_sem=plane_recv_sem.at[slot],
            device_id=at_plane((q + i) % plane),
            device_id_type=MESH,
        )

    def side_copy(kind, direction, src, dst):
        return pltpu.make_async_remote_copy(
            src_ref=src,
            dst_ref=dst.at[q, 1 - direction],
            send_sem=side_send_sem.at[kind, direction],
            recv_sem=side_recv_sem.at[kind, direction],
            device_id=(right, left)[direction],
            device_id_type=MESH,
        )

    def plane_gather_start(src, dst, slot):
        @pl.loop(1, plane)
        def _(i):
            plane_copy(i, src, dst.at[q], slot).start()

    def plane_scatter_start(src, dst, slot):
        @pl.loop(1, plane)
        def _(i):
            plane_copy(i, src.at[(q + i) % plane], dst.at[q], slot).start()

    def plane_wait_recv(dst, slot):
        whole = dst.at[pl.ds(0, plane - 1)]
        pltpu.make_async_copy(whole, whole, plane_recv_sem.at[slot]).wait()

    def plane_wait_send(dst, slot):
        whole = dst.at[pl.ds(0, plane - 1)]
        pltpu.make_async_copy(whole, whole, plane_send_sem.at[slot]).wait()

    def line_copy(i, src, dst, slot):
        return pltpu.make_async_remote_copy(
            src_ref=src,
            dst_ref=dst,
            send_sem=line_send_sem.at[slot],
            recv_sem=line_recv_sem.at[slot],
            device_id=at_chip(chip(i)),
            device_id_type=MESH,
        )

    def line_scatter(total, src, dst, slot):
        share = src.shape[1]
        for i in range(chips):
            src[i] = total[i * share : (i + 1) * share]

        @pl.loop(1, chips)
        def _(i):
            line_copy(i, src.at[chip(i)], dst.at[z], slot).start()

        dst[z] = src[z]

    def line_gather(received, dst, slot):
        line_wait(received, line_recv_sem, slot)
        dst[z] = sum_first(received, chips)

        @pl.loop(1, chips)
        def _(i):
            line_copy(i, dst.at[z], dst.at[z], slot + 1).start()

    def line_finish(gathered, dst, slot):
        line_wait(gathered, line_recv_sem, slot + 1)
        share = gathered.shape[1]
        for i in range(chips):
            dst[q, i * share : (i + 1) * share] = gathered[i]

    def line_wait(buf, sem, slot):
        whole = buf.at[pl.ds(0, chips - 1)]
        pltpu.make_async_copy(whole, whole, sem.at[slot]).wait()

    def sum_first(ref, count):
        total = ref[0]
        for i in range(1, count):
            total = total + ref[i]
        return total

    def ring(kind, direction, n, src, dst):
        return pltpu.make_async_remote_copy(
            src_ref=src,
            dst_ref=dst,
            send_sem=ring_send_sem.at[kind, direction, n],
            recv_sem=ring_recv_sem.at[kind, direction, n],
            device_id=(right, left)[direction],
            device_id_type=MESH,
        )

    def gather_slot(direction, n, shift):
        away = n // 2 + shift
        h = (1 if n % 2 == 0 else 0) if direction == 0 else (0 if n % 2 == 0 else 1)
        return chip(-away if direction == 0 else away), h

    def gather_copy(buf, kind, direction, n):
        at, h = gather_slot(direction, n, 0)
        return ring(kind, direction, n, buf.at[at, h], buf.at[at, h])

    def gather_wait(buf, kind, direction, n):
        at, h = gather_slot(direction, n, 1)
        ring(kind, direction, n, buf.at[at, h], buf.at[at, h]).wait_recv()

    waited = set()

    def gather_need(buf, kind, direction, n):
        if n >= 0 and (kind, direction, n) not in waited:
            waited.add((kind, direction, n))
            gather_wait(buf, kind, direction, n)

    def gather_send(buf, kind, n):
        if n >= steps - 2:
            return
        for direction in range(2):
            if n >= 2:
                gather_need(buf, kind, direction, n - 2)
            gather_copy(buf, kind, direction, n).start()

    def sum_slot(direction, n):
        away = half_ring - (n + 1) // 2
        h = n % 2 if direction == 0 else 1 - n % 2
        return chip(away if direction == 0 else -away), h

    def sum_copy(direction, n):
        at, h = sum_slot(direction, n)
        return ring(1, direction, n, t_part.at[at, h], t_recv.at[direction, n])

    def sum_send(n):
        if n >= steps:
            return
        for direction in range(2):
            if n >= 2:
                sum_copy(direction, n - 2).wait_recv()
                at, h = sum_slot(direction, n)
                t_part[at, h] = t_part[at, h] + t_recv[direction, n - 2]
            sum_copy(direction, n).start()

    def panel_send(n):
        gather_send(p_all, 0, n)

    def image_send(n):
        gather_send(z_all, 2, n)

    def panel_send_part(part):
        share = half // 2
        for direction in range(2):
            at, h = gather_slot(direction, 1, 0)
            place = p_all.at[at, h, pl.ds(part * share, share)]
            ring(0, direction, 1, place, place).start()

    for direction in range(2):
        side_copy(0, direction, p_all.at[z, 0, pl.ds(0, PIECE)], p_side).start()
    panel_send(0)

    @pl.loop(0, chips)
    def _(i):
        a_remote(i).start()

    own = p_all[z].reshape(block, width)
    gram_src[...] = dot(own, own, ((0,), (0,))).reshape(gram_src.shape)
    plane_scatter_start(gram_src, gram_recv, 1)
    gram_recv[q] = gram_src[q]
    plane_gather_start(p_all.at[z, 0, pl.ds(0, PIECE)], p_slab, 0)
    p_slab[q] = p_all[z, 0, 0:PIECE]

    def partial_sums(i):
        target = block_of(i)
        a_local(i).wait()
        pltpu.make_async_remote_copy(
            src_ref=a_buf.at[1 - core, target],
            dst_ref=a_buf.at[1 - core, target],
            send_sem=a_send_sem.at[i],
            recv_sem=a_recv_sem.at[i],
            device_id=sibling,
            device_id_type=MESH,
        ).wait_recv()
        slab = p_slab[...].reshape(plane * PIECE, width)
        both = jnp.concatenate([a_buf[0, target], a_buf[1, target]], axis=1)
        t_part[target] = dot(both, slab).reshape(2, half, width)

    panel_send_part(0)
    plane_wait_recv(gram_recv, 1)
    line_scatter(sum_first(gram_recv, plane), gram_line.at[0], gram_line.at[1], 0)
    panel_send_part(1)
    plane_wait_recv(p_slab, 0)
    partial_sums(0)
    line_gather(gram_line.at[1], gram_line.at[2], 0)
    sum_send(0)

    @pl.loop(1, 3)
    def _(i):
        partial_sums(i)

    sum_send(1)
    panel_send(2)
    line_finish(gram_line.at[2], gram, 0)
    plane_gather_start(gram.at[q], gram, 2)

    @pl.loop(3, chips)
    def _(i):
        partial_sums(i)

    nb = width // 2
    chunk = nb // 4

    def eliminate(first):
        size = nb - first
        lanes = lax.broadcasted_iota(jnp.int32, (1, nb), 1)
        sub = lax.broadcasted_iota(jnp.int32, (size, 1), 0) + first

        @pl.loop(first, first + chunk)
        def _(j):
            pivot_row = work[pl.ds(j, 1), :]
            pick = lanes == j
            pivot = jnp.sum(jnp.where(pick, pivot_row[:, :nb], 0.0), axis=1, keepdims=True)
            body = work[first:, :]
            column = jnp.sum(jnp.where(pick, body[:, :nb], 0.0), axis=1, keepdims=True)
            factor = jnp.where(sub > j, column / pivot, 0.0)
            work[first:, :] = body - factor * pivot_row

    def load_work(matrix):
        row_id = lax.broadcasted_iota(jnp.int32, (nb, nb), 0)
        col_id = lax.broadcasted_iota(jnp.int32, (nb, nb), 1)
        work[:, :nb] = matrix
        work[:, nb:] = jnp.where(row_id == col_id, 1.0, 0.0)

    def factors():
        row_id = lax.broadcasted_iota(jnp.int32, (nb, nb), 0)
        col_id = lax.broadcasted_iota(jnp.int32, (nb, nb), 1)
        upper = work[:, :nb]
        diagonal = jnp.sum(jnp.where(row_id == col_id, upper, 0.0), axis=1, keepdims=True)
        scale = 1.0 / jnp.sqrt(diagonal)
        return jnp.where(col_id >= row_id, upper * scale, 0.0), work[:, nb:] * scale

    sum_send(2)
    for direction in range(2):
        side_copy(0, direction, p_all.at[z, 0, pl.ds(0, PIECE)], p_side).wait_recv()
    plane_gather_start(p_side.at[q], p_side, 6)
    plane_wait_recv(gram, 2)
    gram_rows = gram_src.shape[1]
    whole_gram = gram[...].reshape(plane * gram_rows, width)
    load_work(whole_gram[:nb, :nb])
    eliminate(0)
    eliminate(chunk)
    sum_send(3)
    eliminate(2 * chunk)
    eliminate(3 * chunk)
    sum_send(4)
    upper_a, inverse_a = factors()
    r_ref[:nb, :nb] = upper_a
    lower_inv[:nb, :nb] = inverse_a
    whole_gram = gram[...].reshape(plane * gram_rows, width)
    cross = dot(inverse_a, whole_gram[:nb, nb:])
    r_ref[:nb, nb:] = cross
    r_ref[nb:, :nb] = jnp.zeros((nb, nb), jnp.float32)
    lower_inv[:nb, nb:] = jnp.zeros((nb, nb), jnp.float32)
    load_work(whole_gram[nb:, nb:] - dot(cross, cross, ((0,), (0,))))
    eliminate(0)
    sum_send(5)
    eliminate(chunk)
    sum_send(6)
    eliminate(2 * chunk)
    panel_send(3)
    panel_send(4)
    eliminate(3 * chunk)
    upper_b, inverse_b = factors()
    r_ref[nb:, nb:] = upper_b
    lower_inv[nb:, nb:] = inverse_b
    lower_inv[nb:, :nb] = -dot(inverse_b, dot(r_ref[:nb, nb:], lower_inv[:nb, :nb], ((0,), (0,))))

    slab = plane * PIECE
    inverse = lower_inv[...]
    plane_wait_recv(p_side, 6)

    def columns_of(i):
        return slice(i * slab, (i + 1) * slab)

    def three(own_rows, side):
        return (
            own_rows[...].reshape(slab, width),
            side[:, 0].reshape(slab, width),
            side[:, 1].reshape(slab, width),
        )

    for i, slab_rows in enumerate(three(p_slab, p_side)):
        basis_slab_t[:, columns_of(i)] = dot(inverse, slab_rows, ((1,), (1,)))
    own_basis = dot(p_all[z].reshape(block, width), inverse, ((1,), (1,)))

    for copy in rest_load:
        copy.wait()
    for direction in range(2):
        for n in (steps - 2, steps - 1):
            sum_copy(direction, n).wait_recv()
    for h in range(2):
        first = t_recv[0, steps - 2 if h == 1 else steps - 1]
        second = t_recv[1, steps - 2 if h == 0 else steps - 1]
        total = t_part[z, h] + first + second
        z_all[z, h] = rest[h] + 2.0 * dot(total, inverse, ((1,), (1,)))
    for direction in range(2):
        side_copy(1, direction, z_all.at[z, 0, pl.ds(0, PIECE)], z_side).start()
    image_send(0)
    coup_src[...] = dot(
        own_basis, z_all[z].reshape(block, width), ((0,), (0,))
    ).reshape(coup_src.shape)
    plane_scatter_start(coup_src, coup_recv, 4)
    coup_recv[q] = coup_src[q]
    plane_gather_start(z_all.at[z, 0, pl.ds(0, PIECE)], z_slab, 3)
    z_slab[q] = z_all[z, 0, 0:PIECE]
    plane_wait_recv(coup_recv, 4)
    coup_piece[z] = sum_first(coup_recv, plane)

    @pl.loop(1, chips)
    def _(i):
        line_copy(i, coup_piece.at[z], coup_piece.at[z], 2).start()

    image_send(1)
    for direction in range(2):
        side_copy(1, direction, z_all.at[z, 0, pl.ds(0, PIECE)], z_side).wait_recv()
    plane_gather_start(z_side.at[q], z_side, 7)
    image_send(2)
    line_wait(coup_piece, line_recv_sem, 2)
    coup[q] = sum_first(coup_piece, chips)
    plane_gather_start(coup.at[q], coup, 5)
    image_send(3)
    plane_wait_recv(z_slab, 3)
    plane_wait_recv(z_side, 7)
    plane_wait_recv(coup, 5)
    coupling = coup[...].reshape(width, width)
    for i, slab_rows in enumerate(three(z_slab, z_side)):
        slab_t = basis_slab_t[:, columns_of(i)]
        inner = jnp.transpose(slab_rows)
        inner = inner - dot(coupling, slab_t) - dot(coupling, slab_t, ((0,), (0,)))
        mix[:, columns_of(i)] = dot(lower_inv[...], inner, ((0,), (0,)))

    columns = slab // 2

    def first_row(at, core_of_rows, h):
        return pl.multiple_of((2 * at + core_of_rows) * block + h * half, half)

    def update_block(at, h, i):
        value = dot(p_all[at, h], mix[:, columns_of(i)])
        value = value + dot(z_all[at, h], basis_slab_t[:, columns_of(i)])
        return value[:, :columns], value[:, columns:]

    def swap_copy(slot, start):
        return pltpu.make_async_remote_copy(
            src_ref=staged.at[slot],
            dst_ref=out_ref.at[pl.ds(start, half)],
            send_sem=out_send_sem.at[slot],
            recv_sem=out_recv_sem.at[slot],
            device_id=sibling,
            device_id_type=MESH,
        )

    done = []

    def update(at, h):
        slot = len(done)
        low, high = update_block(at, h, 0)
        staged[slot] = jnp.where(core == 0, high, low)
        start = first_row(at, core, h)
        swap_copy(slot, start).start()
        out_ref[pl.ds(start, half), :] = jnp.where(core == 0, low, high)
        done.append((at, h))

    def pass_copy(direction, n, source, target, at, h):
        return pltpu.make_async_remote_copy(
            src_ref=passed.at[direction, n, target],
            dst_ref=out_ref.at[pl.ds(first_row(at, source, h), half)],
            send_sem=pass_send_sem.at[direction, n, target],
            recv_sem=pass_recv_sem.at[direction, n, source],
            device_id=(r, 2 * chip(1 if direction == 0 else -1) + target),
            device_id_type=MESH,
        )

    def pass_send(n):
        for direction in range(2):
            last = steps - 2 + n
            gather_need(z_all, 2, direction, last - 2)
            gather_need(p_all, 0, direction, last - 2)
            at, h = gather_slot(direction, last, 0)
            low, high = update_block(at, h, 1 + direction)
            passed[direction, n, 0] = low
            passed[direction, n, 1] = high
            for target in range(2):
                pass_copy(direction, n, core, target, at, h).start()

    def update_received(n):
        for direction in range(2):
            gather_need(z_all, 2, direction, n)
            gather_need(p_all, 0, direction, n)
            update(*gather_slot(direction, n, 1))

    update(z, 0)
    update(z, 1)
    update_received(0)
    image_send(4)
    pass_send(0)
    if steps > 4:
        update_received(1)
    pass_send(1)
    for n in range(2, steps - 2):
        update_received(n)

    for direction in range(2):
        for n in range(steps):
            sum_copy(direction, n).wait_send()
        for n in range(steps - 2):
            gather_copy(p_all, 0, direction, n).wait_send()
            gather_copy(z_all, 2, direction, n).wait_send()
        side_copy(0, direction, p_all.at[z, 0, pl.ds(0, PIECE)], p_side).wait_send()
        side_copy(1, direction, z_all.at[z, 0, pl.ds(0, PIECE)], z_side).wait_send()

    @pl.loop(0, chips)
    def _(i):
        a_remote(i).wait_send()

    plane_wait_send(p_slab, 0)
    plane_wait_send(gram_recv, 1)
    plane_wait_send(gram, 2)
    plane_wait_send(z_slab, 3)
    plane_wait_send(coup_recv, 4)
    plane_wait_send(coup, 5)
    plane_wait_send(p_side, 6)
    plane_wait_send(z_side, 7)
    for slot in range(2):
        line_wait(gram_line.at[1], line_send_sem, slot)
    line_wait(coup_piece, line_send_sem, 2)

    for slot, (at, h) in enumerate(done):
        swap_copy(slot, first_row(at, core, h)).wait_send()
        swap_copy(slot, first_row(at, 1 - core, h)).wait_recv()
    for n in range(2):
        for direction in range(2):
            last = steps - 2 + n
            for index in range(2):
                at, h = gather_slot(direction, last, 0)
                pass_copy(direction, n, core, index, at, h).wait_send()
                at, h = gather_slot(direction, last, 1)
                pass_copy(direction, n, index, index, at, h).wait_recv()


def per_device(panel, image_rest, a_slab):
    f32 = jnp.float32
    rows = lax.axis_size("row")
    chips = lax.axis_size("col") // 2
    block, width = panel.shape
    columns = a_slab.shape[1]
    half = block // 2
    plane = 2 * rows
    gram_rows = width // plane
    slab = plane * PIECE
    steps = chips - 1
    dma = pltpu.SemaphoreType.DMA
    hbm = pl.BlockSpec(memory_space=pltpu.HBM)
    vmem = pl.BlockSpec(memory_space=pltpu.VMEM)
    piece = pltpu.VMEM((plane, gram_rows, width), f32)
    gram_line = pltpu.VMEM((3, chips, gram_rows // chips, width), f32)
    coup_piece = pltpu.VMEM((chips, gram_rows, width), f32)
    return pl.pallas_call(
        functools.partial(kernel, rows, chips),
        out_shape=(
            pltpu.VMEM((width, width), f32),
            pltpu.VMEM(a_slab.shape, f32),
        ),
        in_specs=[hbm, hbm, hbm],
        out_specs=(vmem, vmem),
        scratch_shapes=[
            pltpu.VMEM((2, chips, block, columns), f32),
            pltpu.VMEM((chips, 2, half, width), f32),
            pltpu.VMEM((chips, 2, half, width), f32),
            pltpu.VMEM((chips, 2, half, width), f32),
            pltpu.VMEM((2, steps, half, width), f32),
            pltpu.VMEM((2, half, width), f32),
            pltpu.VMEM((plane, PIECE, width), f32),
            pltpu.VMEM((plane, PIECE, width), f32),
            pltpu.VMEM((plane, 2, PIECE, width), f32),
            pltpu.VMEM((plane, 2, PIECE, width), f32),
            piece,
            piece,
            gram_line,
            piece,
            piece,
            piece,
            coup_piece,
            piece,
            pltpu.VMEM((width // 2, width), f32),
            pltpu.VMEM((width, width), f32),
            pltpu.VMEM((width, 3 * slab), f32),
            pltpu.VMEM((width, 3 * slab), f32),
            pltpu.VMEM((2 * chips - 4, half, columns), f32),
            pltpu.VMEM((2, 2, 2, half, columns), f32),
            dma((4,)),
            dma((chips,)),
            dma((chips,)),
            dma((chips,)),
            dma((8,)),
            dma((8,)),
            dma((4,)),
            dma((4,)),
            dma((3, 2, steps)),
            dma((3, 2, steps)),
            dma((2, 2)),
            dma((2, 2)),
            dma((2 * chips - 4,)),
            dma((2 * chips - 4,)),
            dma((2, 2, 2)),
            dma((2, 2, 2)),
        ],
        compiler_params=pltpu.CompilerParams(
            collective_id=0, has_side_effects=True, vmem_limit_bytes=56 * 1024 * 1024
        ),
    )(panel, image_rest, a_slab)


def solution(mesh):
    placed = (P(("row", "col"), None), P(("row", "col"), None), P("row", "col"))
    return jax.shard_map(
        per_device, mesh=mesh, in_specs=placed, out_specs=(P(), P("row", "col")), check_vma=False
    )
```

```python
import functools

import jax
import jax.numpy as jnp
from jax import lax
from jax.experimental import pallas as pl
from jax.experimental.pallas import tpu as pltpu
from jax.sharding import PartitionSpec as P

MESH = pl.DeviceIdType.MESH
HIGHEST = lax.Precision.HIGHEST
PIECE = 8


def dot(left, right, contract=((1,), (0,))):
    return lax.dot_general(
        left, right, (contract, ((), ())), precision=HIGHEST, preferred_element_type=jnp.float32
    )


def kernel(
    rows,
    chips,
    panel_hbm,
    rest_hbm,
    a_hbm,
    r_ref,
    out_ref,
    a_buf,
    p_all,
    z_all,
    t_part,
    t_recv,
    rest,
    p_slab,
    z_slab,
    p_side,
    z_side,
    gram_src,
    gram_recv,
    gram_line,
    gram,
    coup_src,
    coup_recv,
    coup_line,
    coup,
    work,
    lower_inv,
    basis_slab_t,
    mix,
    staged,
    passed,
    local_sem,
    a_local_sem,
    a_send_sem,
    a_recv_sem,
    plane_send_sem,
    plane_recv_sem,
    line_send_sem,
    line_recv_sem,
    ring_send_sem,
    ring_recv_sem,
    side_send_sem,
    side_recv_sem,
    out_send_sem,
    out_recv_sem,
    pass_send_sem,
    pass_recv_sem,
):
    r = lax.axis_index("row")
    c = lax.axis_index("col")
    z = c // 2
    core = c % 2
    plane = 2 * rows
    q = core * rows + r
    half_ring = chips // 2
    half = p_all.shape[2]
    block = 2 * half
    width = p_all.shape[3]
    steps = chips - 1

    def chip(offset):
        return (z + offset + 2 * chips) % chips

    def at_plane(index):
        return (index % rows, 2 * z + index // rows)

    def at_chip(index):
        return (r, 2 * index + core)

    right, left = at_chip(chip(1)), at_chip(chip(-1))
    sibling = (r, 2 * z + (1 - core))

    panel_load = [
        pltpu.make_async_copy(
            panel_hbm.at[pl.ds(h * half, half)], p_all.at[z, h], local_sem.at[h]
        )
        for h in range(2)
    ]
    rest_load = [
        pltpu.make_async_copy(
            rest_hbm.at[pl.ds(h * half, half)], rest.at[h], local_sem.at[2 + h]
        )
        for h in range(2)
    ]

    def block_of(i):
        magnitude = half_ring - (i + 1) // 2
        sign = 1 - 2 * ((i + 1) % 2)
        return chip(jnp.where(i == 0, half_ring, magnitude * sign))

    def a_local(i):
        target = block_of(i)
        start = pl.multiple_of((2 * target + core) * block, block)
        return pltpu.make_async_copy(
            a_hbm.at[pl.ds(start, block)], a_buf.at[core, target], a_local_sem.at[i]
        )

    def a_remote(i):
        target = block_of(i)
        start = pl.multiple_of((2 * target + 1 - core) * block, block)
        return pltpu.make_async_remote_copy(
            src_ref=a_hbm.at[pl.ds(start, block)],
            dst_ref=a_buf.at[core, target],
            send_sem=a_send_sem.at[i],
            recv_sem=a_recv_sem.at[i],
            device_id=sibling,
            device_id_type=MESH,
        )

    for copy in panel_load:
        copy.start()

    barrier = pltpu.get_barrier_semaphore()

    @pl.loop(1, plane)
    def _(i):
        pl.semaphore_signal(
            barrier, inc=1, device_id=at_plane((q + i) % plane), device_id_type=MESH
        )

    @pl.loop(1, chips)
    def _(i):
        pl.semaphore_signal(barrier, inc=1, device_id=at_chip(chip(i)), device_id_type=MESH)

    for copy in rest_load:
        copy.start()

    @pl.loop(0, chips)
    def _(i):
        a_local(i).start()

    for copy in panel_load:
        copy.wait()
    pl.semaphore_wait(barrier, plane - 1 + chips - 1)

    def plane_copy(i, src, dst, slot):
        return pltpu.make_async_remote_copy(
            src_ref=src,
            dst_ref=dst,
            send_sem=plane_send_sem.at[slot],
            recv_sem=plane_recv_sem.at[slot],
            device_id=at_plane((q + i) % plane),
            device_id_type=MESH,
        )

    def side_copy(kind, direction, src, dst):
        return pltpu.make_async_remote_copy(
            src_ref=src,
            dst_ref=dst.at[q, 1 - direction],
            send_sem=side_send_sem.at[kind, direction],
            recv_sem=side_recv_sem.at[kind, direction],
            device_id=(right, left)[direction],
            device_id_type=MESH,
        )

    def plane_gather_start(src, dst, slot):
        @pl.loop(1, plane)
        def _(i):
            plane_copy(i, src, dst.at[q], slot).start()

    def plane_scatter_start(src, dst, slot):
        @pl.loop(1, plane)
        def _(i):
            plane_copy(i, src.at[(q + i) % plane], dst.at[q], slot).start()

    def plane_wait_recv(dst, slot):
        whole = dst.at[pl.ds(0, plane - 1)]
        pltpu.make_async_copy(whole, whole, plane_recv_sem.at[slot]).wait()

    def plane_wait_send(dst, slot):
        whole = dst.at[pl.ds(0, plane - 1)]
        pltpu.make_async_copy(whole, whole, plane_send_sem.at[slot]).wait()

    def line_copy(i, src, dst, slot):
        return pltpu.make_async_remote_copy(
            src_ref=src,
            dst_ref=dst,
            send_sem=line_send_sem.at[slot],
            recv_sem=line_recv_sem.at[slot],
            device_id=at_chip(chip(i)),
            device_id_type=MESH,
        )

    def line_scatter(total, src, dst, slot):
        share = src.shape[1]
        for i in range(chips):
            src[i] = total[i * share : (i + 1) * share]

        @pl.loop(1, chips)
        def _(i):
            line_copy(i, src.at[chip(i)], dst.at[z], slot).start()

        dst[z] = src[z]

    def line_gather(received, dst, slot):
        line_wait(received, line_recv_sem, slot)
        dst[z] = sum_first(received, chips)

        @pl.loop(1, chips)
        def _(i):
            line_copy(i, dst.at[z], dst.at[z], slot + 1).start()

    def line_finish(gathered, dst, slot):
        line_wait(gathered, line_recv_sem, slot + 1)
        share = gathered.shape[1]
        for i in range(chips):
            dst[q, i * share : (i + 1) * share] = gathered[i]

    def line_wait(buf, sem, slot):
        whole = buf.at[pl.ds(0, chips - 1)]
        pltpu.make_async_copy(whole, whole, sem.at[slot]).wait()

    def sum_first(ref, count):
        total = ref[0]
        for i in range(1, count):
            total = total + ref[i]
        return total

    def ring(kind, direction, n, src, dst):
        return pltpu.make_async_remote_copy(
            src_ref=src,
            dst_ref=dst,
            send_sem=ring_send_sem.at[kind, direction, n],
            recv_sem=ring_recv_sem.at[kind, direction, n],
            device_id=(right, left)[direction],
            device_id_type=MESH,
        )

    def gather_slot(direction, n, shift):
        away = n // 2 + shift
        h = (1 if n % 2 == 0 else 0) if direction == 0 else (0 if n % 2 == 0 else 1)
        return chip(-away if direction == 0 else away), h

    def gather_copy(buf, kind, direction, n):
        at, h = gather_slot(direction, n, 0)
        return ring(kind, direction, n, buf.at[at, h], buf.at[at, h])

    def gather_wait(buf, kind, direction, n):
        at, h = gather_slot(direction, n, 1)
        ring(kind, direction, n, buf.at[at, h], buf.at[at, h]).wait_recv()

    waited = set()

    def gather_need(buf, kind, direction, n):
        if n >= 0 and (kind, direction, n) not in waited:
            waited.add((kind, direction, n))
            gather_wait(buf, kind, direction, n)

    def gather_send(buf, kind, n):
        if n >= steps - 2:
            return
        for direction in range(2):
            if n >= 2:
                gather_need(buf, kind, direction, n - 2)
            gather_copy(buf, kind, direction, n).start()

    def sum_slot(direction, n):
        away = half_ring - (n + 1) // 2
        h = n % 2 if direction == 0 else 1 - n % 2
        return chip(away if direction == 0 else -away), h

    def sum_copy(direction, n):
        at, h = sum_slot(direction, n)
        return ring(1, direction, n, t_part.at[at, h], t_recv.at[direction, n])

    def sum_send(n):
        if n >= steps:
            return
        for direction in range(2):
            if n >= 2:
                sum_copy(direction, n - 2).wait_recv()
                at, h = sum_slot(direction, n)
                t_part[at, h] = t_part[at, h] + t_recv[direction, n - 2]
            sum_copy(direction, n).start()

    def panel_send(n):
        gather_send(p_all, 0, n)

    def image_send(n):
        gather_send(z_all, 2, n)

    def panel_send_part(part):
        share = half // 2
        for direction in range(2):
            at, h = gather_slot(direction, 1, 0)
            place = p_all.at[at, h, pl.ds(part * share, share)]
            ring(0, direction, 1, place, place).start()

    for direction in range(2):
        side_copy(0, direction, p_all.at[z, 0, pl.ds(0, PIECE)], p_side).start()
    panel_send(0)

    @pl.loop(0, chips)
    def _(i):
        a_remote(i).start()

    own = p_all[z].reshape(block, width)
    gram_src[...] = dot(own, own, ((0,), (0,))).reshape(gram_src.shape)
    plane_scatter_start(gram_src, gram_recv, 1)
    gram_recv[q] = gram_src[q]
    plane_gather_start(p_all.at[z, 0, pl.ds(0, PIECE)], p_slab, 0)
    p_slab[q] = p_all[z, 0, 0:PIECE]

    def partial_sums(i):
        target = block_of(i)
        a_local(i).wait()
        pltpu.make_async_remote_copy(
            src_ref=a_buf.at[1 - core, target],
            dst_ref=a_buf.at[1 - core, target],
            send_sem=a_send_sem.at[i],
            recv_sem=a_recv_sem.at[i],
            device_id=sibling,
            device_id_type=MESH,
        ).wait_recv()
        slab = p_slab[...].reshape(plane * PIECE, width)
        both = jnp.concatenate([a_buf[0, target], a_buf[1, target]], axis=1)
        t_part[target] = dot(both, slab).reshape(2, half, width)

    panel_send_part(0)
    plane_wait_recv(gram_recv, 1)
    line_scatter(sum_first(gram_recv, plane), gram_line.at[0], gram_line.at[1], 0)
    panel_send_part(1)
    plane_wait_recv(p_slab, 0)
    partial_sums(0)
    line_gather(gram_line.at[1], gram_line.at[2], 0)
    sum_send(0)

    @pl.loop(1, 3)
    def _(i):
        partial_sums(i)

    sum_send(1)
    panel_send(2)
    line_finish(gram_line.at[2], gram, 0)
    plane_gather_start(gram.at[q], gram, 2)

    @pl.loop(3, chips)
    def _(i):
        partial_sums(i)

    nb = width // 2
    chunk = nb // 4

    def eliminate(first):
        size = nb - first
        lanes = lax.broadcasted_iota(jnp.int32, (1, nb), 1)
        sub = lax.broadcasted_iota(jnp.int32, (size, 1), 0) + first

        @pl.loop(first, first + chunk)
        def _(j):
            pivot_row = work[pl.ds(j, 1), :]
            pick = lanes == j
            pivot = jnp.sum(jnp.where(pick, pivot_row[:, :nb], 0.0), axis=1, keepdims=True)
            body = work[first:, :]
            column = jnp.sum(jnp.where(pick, body[:, :nb], 0.0), axis=1, keepdims=True)
            factor = jnp.where(sub > j, column / pivot, 0.0)
            work[first:, :] = body - factor * pivot_row

    def load_work(matrix):
        row_id = lax.broadcasted_iota(jnp.int32, (nb, nb), 0)
        col_id = lax.broadcasted_iota(jnp.int32, (nb, nb), 1)
        work[:, :nb] = matrix
        work[:, nb:] = jnp.where(row_id == col_id, 1.0, 0.0)

    def factors():
        row_id = lax.broadcasted_iota(jnp.int32, (nb, nb), 0)
        col_id = lax.broadcasted_iota(jnp.int32, (nb, nb), 1)
        upper = work[:, :nb]
        diagonal = jnp.sum(jnp.where(row_id == col_id, upper, 0.0), axis=1, keepdims=True)
        scale = 1.0 / jnp.sqrt(diagonal)
        return jnp.where(col_id >= row_id, upper * scale, 0.0), work[:, nb:] * scale

    sum_send(2)
    for direction in range(2):
        side_copy(0, direction, p_all.at[z, 0, pl.ds(0, PIECE)], p_side).wait_recv()
    plane_gather_start(p_side.at[q], p_side, 6)
    plane_wait_recv(gram, 2)
    gram_rows = gram_src.shape[1]
    whole_gram = gram[...].reshape(plane * gram_rows, width)
    load_work(whole_gram[:nb, :nb])
    eliminate(0)
    eliminate(chunk)
    sum_send(3)
    eliminate(2 * chunk)
    eliminate(3 * chunk)
    sum_send(4)
    upper_a, inverse_a = factors()
    r_ref[:nb, :nb] = upper_a
    lower_inv[:nb, :nb] = inverse_a
    whole_gram = gram[...].reshape(plane * gram_rows, width)
    cross = dot(inverse_a, whole_gram[:nb, nb:])
    r_ref[:nb, nb:] = cross
    r_ref[nb:, :nb] = jnp.zeros((nb, nb), jnp.float32)
    lower_inv[:nb, nb:] = jnp.zeros((nb, nb), jnp.float32)
    load_work(whole_gram[nb:, nb:] - dot(cross, cross, ((0,), (0,))))
    eliminate(0)
    sum_send(5)
    eliminate(chunk)
    sum_send(6)
    eliminate(2 * chunk)
    panel_send(3)
    eliminate(3 * chunk)
    upper_b, inverse_b = factors()
    r_ref[nb:, nb:] = upper_b
    lower_inv[nb:, nb:] = inverse_b
    lower_inv[nb:, :nb] = -dot(inverse_b, dot(r_ref[:nb, nb:], lower_inv[:nb, :nb], ((0,), (0,))))

    slab = plane * PIECE
    inverse = lower_inv[...]
    plane_wait_recv(p_side, 6)

    def columns_of(i):
        return slice(i * slab, (i + 1) * slab)

    def three(own_rows, side):
        return (
            own_rows[...].reshape(slab, width),
            side[:, 0].reshape(slab, width),
            side[:, 1].reshape(slab, width),
        )

    for i, slab_rows in enumerate(three(p_slab, p_side)):
        basis_slab_t[:, columns_of(i)] = dot(inverse, slab_rows, ((1,), (1,)))
    own_basis = dot(p_all[z].reshape(block, width), inverse, ((1,), (1,)))

    for copy in rest_load:
        copy.wait()
    for direction in range(2):
        for n in (steps - 2, steps - 1):
            sum_copy(direction, n).wait_recv()
    for h in range(2):
        first = t_recv[0, steps - 2 if h == 1 else steps - 1]
        second = t_recv[1, steps - 2 if h == 0 else steps - 1]
        total = t_part[z, h] + first + second
        z_all[z, h] = rest[h] + 2.0 * dot(total, inverse, ((1,), (1,)))
    for direction in range(2):
        side_copy(1, direction, z_all.at[z, 0, pl.ds(0, PIECE)], z_side).start()
    image_send(0)
    coup_src[...] = dot(
        own_basis, z_all[z].reshape(block, width), ((0,), (0,))
    ).reshape(coup_src.shape)
    plane_scatter_start(coup_src, coup_recv, 4)
    coup_recv[q] = coup_src[q]
    plane_gather_start(z_all.at[z, 0, pl.ds(0, PIECE)], z_slab, 3)
    z_slab[q] = z_all[z, 0, 0:PIECE]
    plane_wait_recv(coup_recv, 4)
    line_scatter(sum_first(coup_recv, plane), coup_line.at[0], coup_line.at[1], 2)
    image_send(1)
    for direction in range(2):
        side_copy(1, direction, z_all.at[z, 0, pl.ds(0, PIECE)], z_side).wait_recv()
    plane_gather_start(z_side.at[q], z_side, 7)
    line_gather(coup_line.at[1], coup_line.at[2], 2)
    panel_send(4)
    image_send(2)
    line_finish(coup_line.at[2], coup, 2)
    plane_gather_start(coup.at[q], coup, 5)
    image_send(3)
    plane_wait_recv(z_slab, 3)
    plane_wait_recv(z_side, 7)
    plane_wait_recv(coup, 5)
    coupling = coup[...].reshape(width, width)
    for i, slab_rows in enumerate(three(z_slab, z_side)):
        slab_t = basis_slab_t[:, columns_of(i)]
        inner = jnp.transpose(slab_rows)
        inner = inner - dot(coupling, slab_t) - dot(coupling, slab_t, ((0,), (0,)))
        mix[:, columns_of(i)] = dot(lower_inv[...], inner, ((0,), (0,)))

    columns = slab // 2

    def first_row(at, core_of_rows, h):
        return pl.multiple_of((2 * at + core_of_rows) * block + h * half, half)

    def update_block(at, h, i):
        value = dot(p_all[at, h], mix[:, columns_of(i)])
        value = value + dot(z_all[at, h], basis_slab_t[:, columns_of(i)])
        return value[:, :columns], value[:, columns:]

    def swap_copy(slot, start):
        return pltpu.make_async_remote_copy(
            src_ref=staged.at[slot],
            dst_ref=out_ref.at[pl.ds(start, half)],
            send_sem=out_send_sem.at[slot],
            recv_sem=out_recv_sem.at[slot],
            device_id=sibling,
            device_id_type=MESH,
        )

    done = []

    def update(at, h):
        slot = len(done)
        low, high = update_block(at, h, 0)
        staged[slot] = jnp.where(core == 0, high, low)
        start = first_row(at, core, h)
        swap_copy(slot, start).start()
        out_ref[pl.ds(start, half), :] = jnp.where(core == 0, low, high)
        done.append((at, h))

    def pass_copy(direction, n, source, target, at, h):
        return pltpu.make_async_remote_copy(
            src_ref=passed.at[direction, n, target],
            dst_ref=out_ref.at[pl.ds(first_row(at, source, h), half)],
            send_sem=pass_send_sem.at[direction, n, target],
            recv_sem=pass_recv_sem.at[direction, n, source],
            device_id=(r, 2 * chip(1 if direction == 0 else -1) + target),
            device_id_type=MESH,
        )

    def pass_send(n):
        for direction in range(2):
            last = steps - 2 + n
            gather_need(z_all, 2, direction, last - 2)
            gather_need(p_all, 0, direction, last - 2)
            at, h = gather_slot(direction, last, 0)
            low, high = update_block(at, h, 1 + direction)
            passed[direction, n, 0] = low
            passed[direction, n, 1] = high
            for target in range(2):
                pass_copy(direction, n, core, target, at, h).start()

    def update_received(n):
        for direction in range(2):
            gather_need(z_all, 2, direction, n)
            gather_need(p_all, 0, direction, n)
            update(*gather_slot(direction, n, 1))

    update(z, 0)
    update(z, 1)
    update_received(0)
    image_send(4)
    pass_send(0)
    if steps > 4:
        update_received(1)
    pass_send(1)
    for n in range(2, steps - 2):
        update_received(n)

    for direction in range(2):
        for n in range(steps):
            sum_copy(direction, n).wait_send()
        for n in range(steps - 2):
            gather_copy(p_all, 0, direction, n).wait_send()
            gather_copy(z_all, 2, direction, n).wait_send()
        side_copy(0, direction, p_all.at[z, 0, pl.ds(0, PIECE)], p_side).wait_send()
        side_copy(1, direction, z_all.at[z, 0, pl.ds(0, PIECE)], z_side).wait_send()

    @pl.loop(0, chips)
    def _(i):
        a_remote(i).wait_send()

    plane_wait_send(p_slab, 0)
    plane_wait_send(gram_recv, 1)
    plane_wait_send(gram, 2)
    plane_wait_send(z_slab, 3)
    plane_wait_send(coup_recv, 4)
    plane_wait_send(coup, 5)
    plane_wait_send(p_side, 6)
    plane_wait_send(z_side, 7)
    for slot in range(2):
        line_wait(gram_line.at[1], line_send_sem, slot)
        line_wait(coup_line.at[1], line_send_sem, 2 + slot)

    for slot, (at, h) in enumerate(done):
        swap_copy(slot, first_row(at, core, h)).wait_send()
        swap_copy(slot, first_row(at, 1 - core, h)).wait_recv()
    for n in range(2):
        for direction in range(2):
            last = steps - 2 + n
            for index in range(2):
                at, h = gather_slot(direction, last, 0)
                pass_copy(direction, n, core, index, at, h).wait_send()
                at, h = gather_slot(direction, last, 1)
                pass_copy(direction, n, index, index, at, h).wait_recv()


def per_device(panel, image_rest, a_slab):
    f32 = jnp.float32
    rows = lax.axis_size("row")
    chips = lax.axis_size("col") // 2
    block, width = panel.shape
    columns = a_slab.shape[1]
    half = block // 2
    plane = 2 * rows
    gram_rows = width // plane
    slab = plane * PIECE
    steps = chips - 1
    dma = pltpu.SemaphoreType.DMA
    hbm = pl.BlockSpec(memory_space=pltpu.HBM)
    vmem = pl.BlockSpec(memory_space=pltpu.VMEM)
    piece = pltpu.VMEM((plane, gram_rows, width), f32)
    gram_line = pltpu.VMEM((3, chips, gram_rows // chips, width), f32)
    return pl.pallas_call(
        functools.partial(kernel, rows, chips),
        out_shape=(
            pltpu.VMEM((width, width), f32),
            pltpu.VMEM(a_slab.shape, f32),
        ),
        in_specs=[hbm, hbm, hbm],
        out_specs=(vmem, vmem),
        scratch_shapes=[
            pltpu.VMEM((2, chips, block, columns), f32),
            pltpu.VMEM((chips, 2, half, width), f32),
            pltpu.VMEM((chips, 2, half, width), f32),
            pltpu.VMEM((chips, 2, half, width), f32),
            pltpu.VMEM((2, steps, half, width), f32),
            pltpu.VMEM((2, half, width), f32),
            pltpu.VMEM((plane, PIECE, width), f32),
            pltpu.VMEM((plane, PIECE, width), f32),
            pltpu.VMEM((plane, 2, PIECE, width), f32),
            pltpu.VMEM((plane, 2, PIECE, width), f32),
            piece,
            piece,
            gram_line,
            piece,
            piece,
            piece,
            gram_line,
            piece,
            pltpu.VMEM((width // 2, width), f32),
            pltpu.VMEM((width, width), f32),
            pltpu.VMEM((width, 3 * slab), f32),
            pltpu.VMEM((width, 3 * slab), f32),
            pltpu.VMEM((2 * chips - 4, half, columns), f32),
            pltpu.VMEM((2, 2, 2, half, columns), f32),
            dma((4,)),
            dma((chips,)),
            dma((chips,)),
            dma((chips,)),
            dma((8,)),
            dma((8,)),
            dma((4,)),
            dma((4,)),
            dma((3, 2, steps)),
            dma((3, 2, steps)),
            dma((2, 2)),
            dma((2, 2)),
            dma((2 * chips - 4,)),
            dma((2 * chips - 4,)),
            dma((2, 2, 2)),
            dma((2, 2, 2)),
        ],
        compiler_params=pltpu.CompilerParams(
            collective_id=0, has_side_effects=True, vmem_limit_bytes=56 * 1024 * 1024
        ),
    )(panel, image_rest, a_slab)


def solution(mesh):
    placed = (P(("row", "col"), None), P(("row", "col"), None), P("row", "col"))
    return jax.shard_map(
        per_device, mesh=mesh, in_specs=placed, out_specs=(P(), P("row", "col")), check_vma=False
    )
```
